256 devices in a mesh: ctx: 64 (over z, y, core), head: 4 (over x).
Axes of the slice: x: 4, y: 4, z: 8, core: 2. Of those that a mesh axis runs over, the one named last changes fastest.
Arguments:
- sec_q: bfloat16 [8192, 1536], P('ctx', 'head'), may hold values from -7 to 7
- sec_k: bfloat16 [8192, 1536], P('ctx', 'head'), may hold values from -6 to 6
- sec_v: bfloat16 [8192, 1536], P('ctx', 'head'), may hold values from -6 to 6
- hist_k: bfloat16 [2048, 1536], P('ctx', 'head'), may hold values from -6 to 6
- hist_v: bfloat16 [2048, 1536], P('ctx', 'head'), may hold values from -6 to 6
- frame_levels: int32 [64, 2], replicated, may hold values from 0 to 2, as said below
- frame_counts: int32 [64], replicated, may hold values from 1 to 2, as said below
- w_out: bfloat16 [1536, 3072], P('head'), may hold values from -0.15625 to 0.15625
- grad_out: bfloat16 [8192, 3072], P('ctx', 'head'), may hold values from -6 to 6
Outputs:
- out: bfloat16 [8192, 3072], P('ctx', 'head')
- grad_sec_q: bfloat16 [8192, 1536], P('ctx', 'head')
- grad_sec_k: bfloat16 [8192, 1536], P('ctx', 'head')
- grad_sec_v: bfloat16 [8192, 1536], P('ctx', 'head')
- grad_hist_k: bfloat16 [2048, 1536], P('ctx', 'head')
- grad_hist_v: bfloat16 [2048, 1536], P('ctx', 'head')
The draws below stay inside these ranges and needn't reach their ends.
Inputs may be any that keep to these rules, and one draw needn't show every extreme that they name: `frame_levels`: only the first frame_counts[o] levels of owner o count; the tokens of one owner never exceed 32, and in every draw some owner has exactly 32. `frame_counts`: in every draw some owner has 2 frames.
All inputs are finite; a program needn't handle non-finite values.
Results may differ from the reference program's by a relative error of at most 0.033.
Values may be sent and summed in bfloat16 or wider, within the bound.
A program may use at most 192 MiB of HBM per device.

```python
import math
import jax
import jax.numpy as jnp
from jax import lax

D = 3072
HEADS = 12
HDIM = 128
FTOK = 16
FMAX = 2
HW = 1536
HCAP = 32
SEC = 8192
HIST = 2048
N_CTX = 64


def shared_keys(key):
    return jax.random.truncated_normal(key, -6.0, 6.0, (SEC, HW), jnp.float32)


def draw_sec_q(key, part):
    key = jax.random.fold_in(key, 11)
    values_drawn = jax.random.truncated_normal(key, -6.0, 6.0, (SEC, HW), jnp.float32)
    return values_drawn.astype(jnp.bfloat16)


def draw_sec_k(key, part):
    shared = shared_keys(key)
    return shared.astype(jnp.bfloat16)


def frame_plan(key):
    key = jax.random.fold_in(key, 23)
    key_levels, key_counts, key_full = jax.random.split(key, 3)
    levels = jax.random.randint(key_levels, (N_CTX, FMAX), 0, 3)
    pick = jax.random.randint(key_counts, (N_CTX,), 0, 4)
    counts = jnp.where(pick > 0, FMAX, 1)
    full_owner = jax.random.randint(key_full, (), 0, N_CTX)
    is_full = jnp.arange(N_CTX) == full_owner
    levels = jnp.where(is_full[:, None], 0, levels)
    counts = jnp.where(is_full, FMAX, counts)
    return (levels.astype(jnp.int32), counts.astype(jnp.int32))


def draw_frame_levels(key, part):
    return frame_plan(key)[0]


def draw_frame_counts(key, part):
    return frame_plan(key)[1]


def block_levels(key, extent, cuts, low, high):
    def one(position, shards_of):
        heights = jax.random.uniform(jax.random.fold_in(jax.random.fold_in(key, 6), position), (shards_of,), jnp.float32, low / len(cuts), high / len(cuts))
        return jnp.repeat(jnp.exp(heights), extent[position] // shards_of).reshape((-1,) + (1,) * (len(extent) - position - 1))

    level = one(*cuts[0])
    for cut in cuts[1:]:
        level = level * one(*cut)
    return level


def centred(own_key, extent, deviation, bound, cuts=(), held_as=jnp.bfloat16):
    loudness = block_levels(own_key, extent, cuts, -0.22, 0.18) if cuts else 1.0
    result = jax.random.normal(own_key, extent, jnp.float32) * deviation * loudness
    return jnp.minimum(jnp.maximum(result, -bound), bound).astype(held_as)


def setup_inputs(seed: int = 0) -> dict:
    key_of = jax.random.split(jax.random.key(seed), 10)
    return {
        "sec_q": draw_sec_q(jax.random.fold_in(key_of[9], 71), 0),
        "sec_k": draw_sec_k(jax.random.fold_in(key_of[9], 71), 0),
        "sec_v": centred(key_of[2], (SEC, HW), 1.0, 6.0, ((0, 64), (1, 4))),
        "hist_k": centred(key_of[3], (HIST, HW), 1.0, 6.0, ((0, 64), (1, 4))),
        "hist_v": centred(key_of[4], (HIST, HW), 1.0, 6.0, ((0, 64), (1, 4))),
        "frame_levels": draw_frame_levels(jax.random.fold_in(key_of[9], 71), 0),
        "frame_counts": draw_frame_counts(jax.random.fold_in(key_of[9], 71), 0),
        "w_out": centred(key_of[7], (HW, D), HW ** -0.5, 0.15625, ((0, 4),)),
        "grad_out": centred(key_of[8], (SEC, D), 1.0, 6.0, ((0, 64), (1, 4))),
    }


NEG_FILL = -1e+30

def owner_token_counts(frame_levels, frame_counts):
    frame_index = jnp.arange(FMAX, dtype=jnp.int32)[None, :]
    per_frame = jnp.where(frame_index < frame_counts[:, None], jnp.right_shift(jnp.int32(FTOK), 2 * frame_levels), 0)
    return lax.optimization_barrier(jnp.sum(per_frame, axis=1)).astype(jnp.int32)

def reference(sec_q, sec_k, sec_v, hist_k, hist_v, frame_levels, frame_counts, w_out, grad_out):
    score_scale = 1.0 / math.sqrt(HDIM)
    owner_tokens = owner_token_counts(frame_levels, frame_counts)
    hist_valid = (jnp.arange(HCAP, dtype=jnp.int32)[None, :] < owner_tokens[:, None]).reshape(HIST)
    key_valid = jnp.concatenate([jnp.ones((SEC,), dtype=bool), hist_valid])
    all_keys = jnp.concatenate([sec_k, hist_k], axis=0)
    all_values = jnp.concatenate([sec_v, hist_v], axis=0)
    d_attn = lax.dot_general(grad_out, w_out, (((1,), (1,)), ((), ())), preferred_element_type=jnp.float32).astype(jnp.bfloat16)
    block_rows = min(512, SEC)
    block_count = SEC // block_rows

    def by_head(stacked):
        return stacked.reshape(stacked.shape[0], HEADS, HDIM).transpose(1, 0, 2)

    def one_head(operands):
        query_h, key_h, value_h, dattn_h = operands

        def block_step(carry_pair, block_pair):
            grad_key, grad_value = carry_pair
            query_b, dattn_b = block_pair
            scores = jnp.dot(query_b, key_h.T, preferred_element_type=jnp.float32) * score_scale
            scores = jnp.where(key_valid[None, :], scores, NEG_FILL)
            row_top = lax.optimization_barrier(jnp.max(scores, axis=1, keepdims=True))
            log_total = row_top + jnp.log(lax.optimization_barrier(jnp.sum(jnp.exp(scores - row_top), axis=1, keepdims=True)))
            prob_b = jnp.where(key_valid[None, :], jnp.exp(scores - log_total), 0.0).astype(jnp.bfloat16)
            attn_b = jnp.dot(prob_b, value_h, preferred_element_type=jnp.float32).astype(jnp.bfloat16)
            row_delta = lax.optimization_barrier(jnp.sum(attn_b.astype(jnp.float32) * dattn_b.astype(jnp.float32), axis=1, keepdims=True))
            dprobs = jnp.dot(dattn_b, value_h.T, preferred_element_type=jnp.float32)
            dscores = (prob_b.astype(jnp.float32) * (dprobs - row_delta)).astype(jnp.bfloat16)
            grad_query = (jnp.dot(dscores, key_h, preferred_element_type=jnp.float32) * score_scale).astype(jnp.bfloat16)
            grad_key = grad_key + jnp.dot(dscores.T, query_b, preferred_element_type=jnp.float32)
            grad_value = grad_value + jnp.dot(prob_b.T, dattn_b, preferred_element_type=jnp.float32)
            return ((grad_key, grad_value), (attn_b, grad_query))
        zero_grads = jnp.zeros((SEC + HIST, HDIM), jnp.float32)
        query_blocks = query_h.reshape(block_count, block_rows, HDIM)
        dattn_blocks = dattn_h.reshape(block_count, block_rows, HDIM)
        sums_pair, outputs_pair = lax.scan(block_step, (zero_grads, zero_grads), (query_blocks, dattn_blocks))
        attn_full = outputs_pair[0].reshape(SEC, HDIM)
        grad_query_full = outputs_pair[1].reshape(SEC, HDIM)
        grad_key_full = (sums_pair[0] * score_scale).astype(jnp.bfloat16)
        grad_value_full = sums_pair[1].astype(jnp.bfloat16)
        return (attn_full, grad_query_full, grad_key_full, grad_value_full)
    results = lax.map(one_head, (by_head(sec_q), by_head(all_keys), by_head(all_values), by_head(d_attn)))

    def merged(stacked):
        return stacked.transpose(1, 0, 2).reshape(stacked.shape[1], HW)
    attn = merged(results[0])
    out = jnp.dot(attn, w_out, preferred_element_type=jnp.float32).astype(jnp.bfloat16)
    grad_sec_q = merged(results[1])
    grad_keys = merged(results[2])
    grad_values = merged(results[3])
    return (out, grad_sec_q, grad_keys[:SEC], grad_values[:SEC], grad_keys[SEC:], grad_values[SEC:])
```

```python
import functools
import math

import jax
import jax.numpy as jnp
from jax import lax
from jax.experimental import pallas as pl
from jax.experimental.pallas import tpu as pltpu
from jax.sharding import PartitionSpec as P

HDIM = 128
FTOK = 16
FMAX = 2
NEG_FILL = -1e30
MESH = pl.DeviceIdType.MESH

NZ, NY, NC, NX = 8, 4, 2, 4
HEADS = 3
ROWS = 128
HCAP = 32
QT = NZ * ROWS
SECT = NY * NC * ROWS
HIST = NY * NC * HCAP
KT = SECT + HIST
CHUNK = 256
NCHUNK = KT // CHUNK
WIDTH = HEADS * HDIM
OCOLS = 768
BF = jnp.bfloat16
F32 = jnp.float32

OFFS = (0, 1, -1, 2, -2, 3, -3, 4)
SLOT = {off: i for i, off in enumerate(OFFS)}
SLOT[-4] = SLOT[4]

SCALE = 1.0 / math.sqrt(HDIM)
SCALE2 = SCALE * math.log2(math.e)


def dot_nn(a, b):
    return lax.dot_general(a, b, (((1,), (0,)), ((), ())), preferred_element_type=F32)


def dot_nt(a, b):
    return lax.dot_general(a, b, (((1,), (1,)), ((), ())), preferred_element_type=F32)


class Sems:
    def __init__(self):
        self.names = {}

    def __call__(self, *name):
        return self.names.setdefault(name, len(self.names))


N_SEMS = 160


def kernel(
    q_ref, k_ref, v_ref, hk_ref, hv_ref, lev_ref, cnt_ref, w_hbm, g_ref,
    out_ref, gq_ref, gk_ref, gv_ref, ghk_ref, ghv_ref,
    q_all, k_all, v_all, kt, vt, w_all, g_all, do_all, dop, bias,
    s_scr, p_scr, o_scr, ds_scr, dq_scr, dkv_scr,
    st, st_recv, ret, ret_recv, cd,
    o_send, o_recv, dq_send, dq_recv,
    r1_sec, r1_hist, t_sec, t_hist, r2_sec, r2_hist,
    po_send, po_recv,
    send_sem, recv_sem, w_sem,
):
    ctx = lax.axis_index("ctx")
    x = lax.axis_index("head")
    core = lax.rem(ctx, NC)
    y = lax.rem(ctx // NC, NY)
    z = ctx // (NC * NY)
    way = 1 - 2 * core

    def at_z(off):
        return (lax.rem(z + off * way + 2 * NZ, NZ) * NY + y) * NC + core

    def at_y(dy):
        return (z * NY + lax.rem(y + dy, NY)) * NC + core

    def at_x(dx):
        return lax.rem(x + dx, NX)

    sibling = (z * NY + y) * NC + (1 - core)

    sems = Sems()
    sent = []

    def send(src, dst, name, to_ctx=None, to_head=None):
        i = sems(*name)
        copy = pltpu.make_async_remote_copy(
            src_ref=src, dst_ref=dst, send_sem=send_sem.at[i], recv_sem=recv_sem.at[i],
            device_id=(ctx if to_ctx is None else to_ctx, x if to_head is None else to_head),
            device_id_type=MESH,
        )
        copy.start()
        sent.append(copy)

    def recv(dst, name):
        i = sems(*name)
        pltpu.make_async_remote_copy(
            src_ref=dst, dst_ref=dst, send_sem=send_sem.at[i], recv_sem=recv_sem.at[i],
            device_id=(sibling, x), device_id_type=MESH,
        ).wait_recv()

    barrier = pltpu.get_barrier_semaphore()
    peers = [(at_z(o), x) for o in OFFS[1:]]
    peers += [(at_y(d), x) for d in range(1, NY)]
    peers += [(sibling, x)]
    peers += [(ctx, at_x(d)) for d in range(1, NX)]
    for peer in peers:
        pl.semaphore_signal(barrier, inc=1, device_id=peer, device_id_type=MESH)

    w_copy = pltpu.make_async_copy(w_hbm, w_all, w_sem)
    w_copy.start()
    for h in range(HEADS):
        cols = slice(h * HDIM, (h + 1) * HDIM)
        q_all[h, 0:ROWS, :] = q_ref[:, cols]
        k_all[h, 0:ROWS, :] = k_ref[:, cols]
        k_all[h, SECT : SECT + HCAP, :] = hk_ref[:, cols]
        v_all[h, 0:ROWS, :] = v_ref[:, cols]
        v_all[h, SECT : SECT + HCAP, :] = hv_ref[:, cols]

    pl.semaphore_wait(barrier, len(peers))

    def ring_send(buf, tag, off, up):
        there = off - 1 if up else off + 1
        src = buf.at[:, pl.ds(SLOT[off] * ROWS, ROWS), :]
        dst = buf.at[:, pl.ds(SLOT[there] * ROWS, ROWS), :]
        send(src, dst, (tag, there), to_ctx=at_z(1 if up else -1))

    def ring_recv(buf, tag, off):
        recv(buf.at[:, pl.ds(SLOT[off] * ROWS, ROWS), :], (tag, off))

    def gather_step(buf, tag, step):
        if step > 1:
            ring_recv(buf, tag, step - 1)
        ring_send(buf, tag, step - 1, False)
        if step < 4:
            if step > 1:
                ring_recv(buf, tag, 1 - step)
            ring_send(buf, tag, 1 - step, True)

    gather_step(q_all, "q", 1)
    for dx in range(1, NX):
        there = (NX - dx) % NX
        send(g_ref, g_all.at[there], ("g", there), to_head=at_x(dx))
    pieces = ((0, ROWS), (SECT, HCAP))
    for tag, buf in (("k", k_all), ("v", v_all)):
        for dy in (1, 3, 2):
            there = (NY - dy) % NY
            for start, size in pieces:
                src = buf.at[:, pl.ds(start, size), :]
                dst = buf.at[:, pl.ds(start + there * size, size), :]
                send(src, dst, (tag, there, start), to_ctx=at_y(dy))

    def to_sibling(tag, buf):
        for dy in (1, 3, 2):
            for start, size in pieces:
                recv(buf.at[:, pl.ds(start + dy * size, size), :], (tag, dy, start))
        for start, size in pieces:
            src = buf.at[:, pl.ds(start, NY * size), :]
            dst = buf.at[:, pl.ds(start + NY * size, NY * size), :]
            send(src, dst, (tag, "sib", start), to_ctx=sibling)

    def from_sibling(tag, buf):
        for start, size in pieces:
            recv(buf.at[:, pl.ds(start + NY * size, NY * size), :], (tag, "sib", start))

    row = lax.broadcasted_iota(jnp.int32, (HIST, CHUNK), 0)
    limit = jnp.zeros((HIST, CHUNK), jnp.int32)
    for dc in range(NC):
        for dy in range(NY):
            owner = (z * NY + lax.rem(y + dy, NY)) * NC + (core if dc == 0 else 1 - core)
            tokens = jnp.int32(0)
            for f in range(FMAX):
                level = lev_ref[owner, f]
                size = lax.shift_right_logical(jnp.int32(FTOK), 2 * level)
                tokens = tokens + jnp.where(f < cnt_ref[owner], size, 0)
            j = dc * NY + dy
            mine = (row >= j * HCAP) & (row < (j + 1) * HCAP)
            limit = jnp.where(mine, tokens + j * HCAP, limit)
    bias[...] = jnp.where(row < limit, 0.0, NEG_FILL)

    gather_step(q_all, "q", 2)
    to_sibling("k", k_all)
    gather_step(q_all, "q", 3)

    w_copy.wait()

    def w_cols(dx):
        return w_all[:, pl.ds(pl.multiple_of(at_x(dx) * OCOLS, OCOLS), OCOLS)]

    d_attn = dot_nt(g_ref[...], w_cols(0))
    to_sibling("v", v_all)
    for dx in (1, 3, 2):
        recv(g_all.at[dx], ("g", dx))
        d_attn += dot_nt(g_all[dx], w_cols(dx))
    for h in range(HEADS):
        do_all[h, 0:ROWS, :] = d_attn[:, h * HDIM : (h + 1) * HDIM].astype(BF)
    gather_step(do_all, "d", 1)
    gather_step(q_all, "q", 4)

    from_sibling("k", k_all)
    from_sibling("v", v_all)

    def turn(h, _):
        for i in range(KT // HDIM):
            rows = slice(i * HDIM, (i + 1) * HDIM)
            vt[h, :, rows] = v_all[h, rows, :].T
            kt[h, :, rows] = k_all[h, rows, :].T
        return 0

    lax.fori_loop(0, HEADS, turn, 0)

    def forward(pair):
        cols = slice(pair * CHUNK, (pair + 1) * CHUNK)

        def one(h, _):
            query = q_all[h, cols, :]
            top = None
            for c in range(NCHUNK):
                rows = slice(c * CHUNK, (c + 1) * CHUNK)
                s = dot_nt(k_all[h, rows, :], query)
                if c == NCHUNK - 1:
                    s = s + bias[...]
                s_scr[rows, :] = s
                part = jnp.max(s.reshape(CHUNK // 8, 8, CHUNK), axis=0)
                top = part if top is None else jnp.maximum(top, part)
            top = jnp.max(top, axis=0, keepdims=True) * SCALE2
            total = jnp.zeros((8, CHUNK), F32)
            for c in range(NCHUNK):
                rows = slice(c * CHUNK, (c + 1) * CHUNK)
                p = jnp.exp2(s_scr[rows, :] * SCALE2 - top)
                total += jnp.sum(p.reshape(CHUNK // 8, 8, CHUNK), axis=0)
                p_scr[h, rows, cols] = p.astype(BF)
            total = jnp.sum(total, axis=0, keepdims=True)
            o_scr[h, :, cols] = dot_nn(vt[h], p_scr[h, :, cols])
            for i in range(2):
                half = slice(i * ROWS, (i + 1) * ROWS)
                st[2 * pair + i, pl.ds(h, 1), :] = top[:, half]
                st[2 * pair + i, pl.ds(HEADS + h, 1), :] = total[:, half]
            return 0

        lax.fori_loop(0, HEADS, one, 0)

    forward(0)
    forward(1)
    gather_step(do_all, "d", 2)
    forward(2)
    gather_step(do_all, "d", 3)
    ring_recv(q_all, "q", -3)
    ring_recv(q_all, "q", 4)
    forward(3)
    gather_step(do_all, "d", 4)

    eye = lax.broadcasted_iota(jnp.int32, (ROWS, ROWS), 0) == lax.broadcasted_iota(
        jnp.int32, (ROWS, ROWS), 1
    )

    def share(slot):
        rows = slice(slot * ROWS, (slot + 1) * ROWS)
        for h in range(HEADS):
            both = dot_nn(do_all[h, rows, :], o_scr[h, :, rows].astype(BF))
            st[slot, 2 * HEADS + h : 2 * HEADS + h + 1, :] = jnp.sum(
                jnp.where(eye, both, 0.0), axis=0, keepdims=True
            )

    for off in OFFS:
        if off in (-3, 4):
            ring_recv(do_all, "d", off)
        share(SLOT[off])
        if off != 0:
            there = SLOT[-off]
            send(st.at[SLOT[off]], st_recv.at[there], ("st", there), to_ctx=at_z(off))
    for slot in range(1, NZ):
        recv(st_recv.at[slot], ("st", slot))
    parts = [st[0]] + [st_recv[slot] for slot in range(1, NZ)]
    peak = functools.reduce(jnp.maximum, [p[0:HEADS] for p in parts])
    weights = [jnp.exp2(p[0:HEADS] - peak) for p in parts]
    whole = sum(w * p[HEADS : 2 * HEADS] for w, p in zip(weights, parts))
    delta = sum(w * p[2 * HEADS : 3 * HEADS] for w, p in zip(weights, parts)) / whole
    ret[0:HEADS, :] = peak + jnp.log2(whole)
    ret[HEADS : 2 * HEADS, :] = delta
    for off in OFFS[1:]:
        there = SLOT[-off]
        send(ret, ret_recv.at[there], ("ret", there), to_ctx=at_z(off))

    def settle(slot):
        back = ret[...] if slot == 0 else ret_recv[slot]
        factor = jnp.exp2(st[slot, 0:HEADS, :] - back[0:HEADS])
        cd[slot, 0:HEADS, :] = factor
        cd[slot, HEADS : 2 * HEADS, :] = factor * back[HEADS : 2 * HEADS]
        rows = slice(slot * ROWS, (slot + 1) * ROWS)
        for h in range(HEADS):
            column = jnp.broadcast_to(factor[h : h + 1], (ROWS, ROWS)).T
            dop[h, rows, :] = (do_all[h, rows, :].astype(F32) * column).astype(BF)

    for slot in range(NZ):
        if slot:
            recv(ret_recv.at[slot], ("ret", slot))
        settle(slot)

    class RingSum:
        def __init__(self, tag, term, out_buf, in_buf):
            self.tag, self.term, self.out_buf, self.in_buf = tag, term, out_buf, in_buf

        def pass_on(self, off, up, first):
            i = off - 1 if up else 3 - off
            value = self.term(off)
            if not first:
                j = SLOT[off] if up else SLOT[off]
                recv(self.in_buf.at[j], (self.tag, up, off))
                value = value + self.in_buf[j].astype(F32)
            slot = SLOT[off]
            self.out_buf[slot] = value.astype(BF)
            there = off - 1 if up else off + 1
            to = SLOT[4] if there == 0 and not up else SLOT[there]
            send(
                self.out_buf.at[slot], self.in_buf.at[to], (self.tag, up, there),
                to_ctx=at_z(1 if up else -1),
            )

        def step(self, n):
            self.pass_on(5 - n, True, n == 1)
            if n < 4:
                self.pass_on(n - 4, False, n == 1)

        def finish(self):
            recv(self.in_buf.at[SLOT[0]], (self.tag, True, 0))
            recv(self.in_buf.at[SLOT[4]], (self.tag, False, 0))
            both = self.in_buf[SLOT[0]].astype(F32) + self.in_buf[SLOT[4]].astype(F32)
            return self.term(0) + both

    def o_term(off):
        slot = SLOT[off]
        rows = slice(slot * ROWS, (slot + 1) * ROWS)
        return jnp.stack([o_scr[h, :, rows] * cd[slot, h : h + 1, :] for h in range(HEADS)])

    def dq_term(h):
        def term(off):
            slot = SLOT[off]
            return dq_scr[h, :, slot * ROWS : (slot + 1) * ROWS]

        return term

    o_sum = RingSum("o", o_term, o_send, o_recv)
    dq_sums = [RingSum("dq%d" % h, dq_term(h), dq_send.at[h], dq_recv.at[h]) for h in range(HEADS)]

    def backward_keys(h, first, last):
        def one(c, _):
            rows = pl.ds(pl.multiple_of(c * CHUNK, CHUNK), CHUNK)
            value = v_all[h, rows, :]
            for pair in range(4):
                cols = slice(pair * CHUNK, (pair + 1) * CHUNK)
                dp = dot_nt(value, dop[h, cols, :])
                a, b = 2 * pair, 2 * pair + 1
                d = HEADS + h
                minus = jnp.concatenate([cd[a, d : d + 1, :], cd[b, d : d + 1, :]], axis=1)
                ds = p_scr[h, rows, cols].astype(F32) * (dp - minus)
                ds_scr[rows, cols] = ds.astype(BF)
            dkv_scr[h, rows, 0:HDIM] = dot_nn(ds_scr[rows, :], q_all[h]).astype(BF)
            dkv_scr[h, rows, HDIM : 2 * HDIM] = dot_nn(p_scr[h, rows, :], dop[h]).astype(BF)
            return 0

        lax.fori_loop(first, last, one, 0)

    def backward_queries(h):
        for pair in range(4):
            cols = slice(pair * CHUNK, (pair + 1) * CHUNK)
            dq_scr[h, :, cols] = dot_nn(kt[h], ds_scr[:, cols])

    def keys_to_sibling(h):
        send(dkv_scr.at[h, pl.ds(SECT // 2, SECT // 2)], r1_sec.at[h], ("r1s", h), to_ctx=sibling)
        src = dkv_scr.at[h, pl.ds(SECT + HIST // 2, HIST // 2)]
        send(src, r1_hist.at[h], ("r1h", h), to_ctx=sibling)

    def keys_along_y(h):
        recv(r1_sec.at[h], ("r1s", h))
        recv(r1_hist.at[h], ("r1h", h))
        for dy in (1, 3, 2, 0):
            there = (NY - dy) % NY
            for name, mine, got, total, into, start, size in (
                ("r2s", dkv_scr, r1_sec, t_sec, r2_sec, 0, ROWS),
                ("r2h", dkv_scr, r1_hist, t_hist, r2_hist, SECT, HCAP),
            ):
                rows = slice(dy * size, (dy + 1) * size)
                own = mine[h, start + dy * size : start + (dy + 1) * size, :].astype(F32)
                total[h, rows, :] = (own + got[h, rows, :].astype(F32)).astype(BF)
                if dy:
                    src = total.at[h, pl.ds(dy * size, size)]
                    send(src, into.at[h, there], (name, h, there), to_ctx=at_y(dy))

    def keys_finish(h):
        cols = slice(h * HDIM, (h + 1) * HDIM)
        for name, total, into, size, k_out, v_out in (
            ("r2s", t_sec, r2_sec, ROWS, gk_ref, gv_ref),
            ("r2h", t_hist, r2_hist, HCAP, ghk_ref, ghv_ref),
        ):
            value = total[h, 0:size, :].astype(F32)
            for dy in range(1, NY):
                recv(into.at[h, dy], (name, h, dy))
                value = value + into[h, dy].astype(F32)
            k_out[:, cols] = (value[:, 0:HDIM] * SCALE).astype(BF)
            v_out[:, cols] = value[:, HDIM : 2 * HDIM].astype(BF)

    def queries_finish(h):
        total = dq_sums[h].finish() * SCALE
        gq_ref[:, h * HDIM : (h + 1) * HDIM] = total.T.astype(BF)

    o_sum.step(1)
    backward_keys(0, 0, 3)
    o_sum.step(2)
    backward_keys(0, 3, 5)
    backward_queries(0)
    keys_to_sibling(0)
    dq_sums[0].step(1)
    o_sum.step(3)
    backward_keys(1, 0, 3)
    dq_sums[0].step(2)
    o_sum.step(4)
    keys_along_y(0)
    backward_keys(1, 3, 5)
    backward_queries(1)
    keys_to_sibling(1)
    dq_sums[1].step(1)
    dq_sums[0].step(3)
    total_o = o_sum.finish()
    attn = jnp.concatenate([total_o[h].T for h in range(HEADS)], axis=1).astype(BF)
    for dx in (2, 1, 3):
        there = (NX - dx) % NX
        po_send[dx] = dot_nn(attn, w_cols(dx)).astype(BF)
        send(po_send.at[dx], po_recv.at[there], ("po", there), to_head=at_x(dx))
    own_out = dot_nn(attn, w_cols(0))
    backward_keys(2, 0, 3)
    dq_sums[0].step(4)
    dq_sums[1].step(2)
    keys_along_y(1)
    keys_finish(0)
    backward_keys(2, 3, 5)
    backward_queries(2)
    keys_to_sibling(2)
    dq_sums[2].step(1)
    dq_sums[1].step(3)
    queries_finish(0)
    keys_along_y(2)
    dq_sums[2].step(2)
    dq_sums[1].step(4)
    keys_finish(1)
    dq_sums[2].step(3)
    queries_finish(1)
    dq_sums[2].step(4)
    for dx in (1, 3, 2):
        recv(po_recv.at[dx], ("po", dx))
        own_out += po_recv[dx].astype(F32)
    out_ref[...] = own_out.astype(BF)
    keys_finish(2)
    queries_finish(2)

    for copy in sent:
        copy.wait_send()
    assert len(sems.names) <= N_SEMS, len(sems.names)


def shards(sec_q, sec_k, sec_v, hist_k, hist_v, frame_levels, frame_counts, w_out, grad_out):
    vmem = pl.BlockSpec(memory_space=pltpu.VMEM)
    smem = pl.BlockSpec(memory_space=pltpu.SMEM)
    anywhere = pl.BlockSpec(memory_space=pl.ANY)
    scratch = [
        pltpu.VMEM((HEADS, QT, HDIM), BF),
        pltpu.VMEM((HEADS, KT, HDIM), BF),
        pltpu.VMEM((HEADS, KT, HDIM), BF),
        pltpu.VMEM((HEADS, HDIM, KT), BF),
        pltpu.VMEM((HEADS, HDIM, KT), BF),
        pltpu.VMEM((WIDTH, NX * OCOLS), BF),
        pltpu.VMEM((NX, ROWS, OCOLS), BF),
        pltpu.VMEM((HEADS, QT, HDIM), BF),
        pltpu.VMEM((HEADS, QT, HDIM), BF),
        pltpu.VMEM((HIST, CHUNK), F32),
        pltpu.VMEM((KT, CHUNK), F32),
        pltpu.VMEM((HEADS, KT, QT), BF),
        pltpu.VMEM((HEADS, HDIM, QT), F32),
        pltpu.VMEM((KT, QT), BF),
        pltpu.VMEM((HEADS, HDIM, QT), F32),
        pltpu.VMEM((HEADS, KT, 2 * HDIM), BF),
        pltpu.VMEM((NZ, 16, ROWS), F32),
        pltpu.VMEM((NZ, 16, ROWS), F32),
        pltpu.VMEM((8, ROWS), F32),
        pltpu.VMEM((NZ, 8, ROWS), F32),
        pltpu.VMEM((NZ, 8, ROWS), F32),
        pltpu.VMEM((NZ, HEADS, HDIM, ROWS), BF),
        pltpu.VMEM((NZ, HEADS, HDIM, ROWS), BF),
        pltpu.VMEM((HEADS, NZ, HDIM, ROWS), BF),
        pltpu.VMEM((HEADS, NZ, HDIM, ROWS), BF),
        pltpu.VMEM((HEADS, SECT // 2, 2 * HDIM), BF),
        pltpu.VMEM((HEADS, HIST // 2, 2 * HDIM), BF),
        pltpu.VMEM((HEADS, SECT // 2, 2 * HDIM), BF),
        pltpu.VMEM((HEADS, HIST // 2, 2 * HDIM), BF),
        pltpu.VMEM((HEADS, NY, ROWS, 2 * HDIM), BF),
        pltpu.VMEM((HEADS, NY, HCAP, 2 * HDIM), BF),
        pltpu.VMEM((NX, ROWS, OCOLS), BF),
        pltpu.VMEM((NX, ROWS, OCOLS), BF),
        pltpu.SemaphoreType.DMA((N_SEMS,)),
        pltpu.SemaphoreType.DMA((N_SEMS,)),
        pltpu.SemaphoreType.DMA(()),
    ]
    shapes = [
        jax.ShapeDtypeStruct((ROWS, OCOLS), BF),
        jax.ShapeDtypeStruct((ROWS, WIDTH), BF),
        jax.ShapeDtypeStruct((ROWS, WIDTH), BF),
        jax.ShapeDtypeStruct((ROWS, WIDTH), BF),
        jax.ShapeDtypeStruct((HCAP, WIDTH), BF),
        jax.ShapeDtypeStruct((HCAP, WIDTH), BF),
    ]
    return pl.pallas_call(
        kernel,
        out_shape=shapes,
        in_specs=[vmem] * 5 + [smem] * 2 + [anywhere, vmem],
        out_specs=[vmem] * 6,
        scratch_shapes=scratch,
        compiler_params=pltpu.CompilerParams(
            collective_id=0, has_side_effects=True, vmem_limit_bytes=60 * 1024 * 1024
        ),
    )(sec_q, sec_k, sec_v, hist_k, hist_v, frame_levels, frame_counts, w_out, grad_out)


def solution(mesh):
    both = P("ctx", "head")
    placed = (both, both, both, both, both, P(), P(), P("head", None), both)
    return jax.shard_map(
        shards, mesh=mesh, in_specs=placed, out_specs=(both,) * 6, check_vma=False
    )
```

```python
import functools
import math

import jax
import jax.numpy as jnp
from jax import lax
from jax.experimental import pallas as pl
from jax.experimental.pallas import tpu as pltpu
from jax.sharding import PartitionSpec as P

HDIM = 128
FTOK = 16
FMAX = 2
NEG_FILL = -1e30
MESH = pl.DeviceIdType.MESH

NZ, NY, NC, NX = 8, 4, 2, 4
HEADS = 3
ROWS = 128
HCAP = 32
QT = NZ * ROWS
SECT = NY * NC * ROWS
HIST = NY * NC * HCAP
KT = SECT + HIST
CHUNK = 256
NCHUNK = KT // CHUNK
WIDTH = HEADS * HDIM
OCOLS = 768
BF = jnp.bfloat16
F32 = jnp.float32

OFFS = (0, 1, -1, 2, -2, 3, -3, 4)
SLOT = {off: i for i, off in enumerate(OFFS)}
SLOT[-4] = SLOT[4]

SCALE = 1.0 / math.sqrt(HDIM)
SCALE2 = SCALE * math.log2(math.e)


def dot_nn(a, b):
    return lax.dot_general(a, b, (((1,), (0,)), ((), ())), preferred_element_type=F32)


def dot_nt(a, b):
    return lax.dot_general(a, b, (((1,), (1,)), ((), ())), preferred_element_type=F32)


class Sems:
    def __init__(self):
        self.names = {}

    def __call__(self, *name):
        return self.names.setdefault(name, len(self.names))


N_SEMS = 224


def kernel(
    q_ref, k_ref, v_ref, hk_ref, hv_ref, lev_ref, cnt_ref, w_hbm, g_ref,
    out_ref, gq_ref, gk_ref, gv_ref, ghk_ref, ghv_ref,
    q_all, kv_all, kt, vt, w_all, g_all, do_all, dop, bias,
    s_scr, p_scr, o_part, ds_scr, dq_part, dkv_scr,
    st, ret, ret_recv, cd,
    o_mid, o_in, st_mid, st_in, dq_mid, dq_in,
    r1_sec, r1_hist, t_sec, t_hist, r2_sec, r2_hist,
    po_send, po_recv,
    send_sem, recv_sem, w_sem,
):
    ctx = lax.axis_index("ctx")
    x = lax.axis_index("head")
    core = lax.rem(ctx, NC)
    y = lax.rem(ctx // NC, NY)
    z = ctx // (NC * NY)
    way = 1 - 2 * core

    def at_z(off):
        return (lax.rem(z + off * way + 2 * NZ, NZ) * NY + y) * NC + core

    def at_y(dy):
        return (z * NY + lax.rem(y + dy, NY)) * NC + core

    def at_x(dx):
        return lax.rem(x + dx, NX)

    sibling = (z * NY + y) * NC + (1 - core)

    sems = Sems()
    sent = []

    def send(src, dst, name, to_ctx=None, to_head=None):
        i = sems(*name)
        copy = pltpu.make_async_remote_copy(
            src_ref=src, dst_ref=dst, send_sem=send_sem.at[i], recv_sem=recv_sem.at[i],
            device_id=(ctx if to_ctx is None else to_ctx, x if to_head is None else to_head),
            device_id_type=MESH,
        )
        copy.start()
        sent.append(copy)

    def recv(dst, name):
        i = sems(*name)
        pltpu.make_async_remote_copy(
            src_ref=dst, dst_ref=dst, send_sem=send_sem.at[i], recv_sem=recv_sem.at[i],
            device_id=(sibling, x), device_id_type=MESH,
        ).wait_recv()

    barrier = pltpu.get_barrier_semaphore()
    peers = [(at_z(o), x) for o in OFFS[1:]]
    peers += [(at_y(d), x) for d in range(1, NY)]
    peers += [(sibling, x)]
    peers += [(ctx, at_x(d)) for d in range(1, NX)]
    for peer in peers:
        pl.semaphore_signal(barrier, inc=1, device_id=peer, device_id_type=MESH)

    w_copy = pltpu.make_async_copy(w_hbm, w_all, w_sem)
    w_copy.start()
    for h in range(HEADS):
        cols = slice(h * HDIM, (h + 1) * HDIM)
        q_all[h, 0:ROWS, :] = q_ref[:, cols]
        kv_all[h, 0, 0:ROWS, :] = k_ref[:, cols]
        kv_all[h, 0, SECT : SECT + HCAP, :] = hk_ref[:, cols]
        kv_all[h, 1, 0:ROWS, :] = v_ref[:, cols]
        kv_all[h, 1, SECT : SECT + HCAP, :] = hv_ref[:, cols]

    pl.semaphore_wait(barrier, len(peers))

    def z_slot(buf, h, off):
        return buf.at[h, pl.ds(SLOT[off] * ROWS, ROWS), :]

    def z_send(buf, tag, h, off, there, to):
        send(z_slot(buf, h, off), z_slot(buf, h, there), (tag, h, there), to_ctx=at_z(to))

    def z_recv(buf, tag, h, *offs):
        for off in offs:
            recv(z_slot(buf, h, off), (tag, h, off))

    def z_first(buf, tag, h):
        for off in (2, -2, 1, -1):
            z_send(buf, tag, h, 0, -off, off)

    def z_second(buf, tag, h):
        z_recv(buf, tag, h, 2)
        z_send(buf, tag, h, 2, 4, -2)
        z_send(buf, tag, h, 2, 3, -1)
        z_recv(buf, tag, h, -2)
        z_send(buf, tag, h, -2, -3, 1)

    def z_rest(buf, tag, h):
        z_recv(buf, tag, h, 1, -1, 3, -3, 4)

    pieces = ((0, ROWS), (SECT, HCAP))

    def kv_first(h):
        for dy in (2, 1, 3):
            there = (NY - dy) % NY
            for start, size in pieces:
                src = kv_all.at[h, :, pl.ds(start, size), :]
                dst = kv_all.at[h, :, pl.ds(start + there * size, size), :]
                send(src, dst, ("kv", h, there, start), to_ctx=at_y(dy))

    def kv_second(h):
        for dy in (1, 3, 2):
            for start, size in pieces:
                recv(kv_all.at[h, :, pl.ds(start + dy * size, size), :], ("kv", h, dy, start))
        for start, size in pieces:
            src = kv_all.at[h, :, pl.ds(start, NY * size), :]
            dst = kv_all.at[h, :, pl.ds(start + NY * size, NY * size), :]
            send(src, dst, ("kv", h, "sib", start), to_ctx=sibling)

    def kv_rest(h):
        for start, size in pieces:
            dst = kv_all.at[h, :, pl.ds(start + NY * size, NY * size), :]
            recv(dst, ("kv", h, "sib", start))
        for i in range(KT // HDIM):
            rows = slice(i * HDIM, (i + 1) * HDIM)
            kt[h, :, rows] = kv_all[h, 0, rows, :].T
            vt[h, :, rows] = kv_all[h, 1, rows, :].T

    for dx in (2, 1, 3):
        there = (NX - dx) % NX
        send(g_ref, g_all.at[there], ("g", there), to_head=at_x(dx))
    for h in range(HEADS):
        kv_first(h)
        z_first(q_all, "q", h)

    row = lax.broadcasted_iota(jnp.int32, (HIST, CHUNK), 0)
    limit = jnp.zeros((HIST, CHUNK), jnp.int32)
    for dc in range(NC):
        for dy in range(NY):
            owner = (z * NY + lax.rem(y + dy, NY)) * NC + (core if dc == 0 else 1 - core)
            tokens = jnp.int32(0)
            for f in range(FMAX):
                level = lev_ref[f, owner]
                size = lax.shift_right_logical(jnp.int32(FTOK), 2 * level)
                tokens = tokens + jnp.where(f < cnt_ref[owner], size, 0)
            j = dc * NY + dy
            mine = (row >= j * HCAP) & (row < (j + 1) * HCAP)
            limit = jnp.where(mine, tokens + j * HCAP, limit)
    bias[...] = jnp.where(row < limit, 0.0, NEG_FILL)

    def w_cols(dx):
        return w_all[:, pl.ds(pl.multiple_of(at_x(dx) * OCOLS, OCOLS), OCOLS)]

    def cotangent():
        w_copy.wait()
        d_attn = dot_nt(g_ref[...], w_cols(0))
        for dx in (1, 3, 2):
            recv(g_all.at[dx], ("g", dx))
            d_attn += dot_nt(g_all[dx], w_cols(dx))
        for h in range(HEADS):
            do_all[h, 0:ROWS, :] = d_attn[:, h * HDIM : (h + 1) * HDIM].astype(BF)
            z_first(do_all, "d", h)

    def forward(h, pair):
        cols = slice(pair * CHUNK, (pair + 1) * CHUNK)
        query = q_all[h, cols, :]
        top = None
        for c in range(NCHUNK):
            rows = slice(c * CHUNK, (c + 1) * CHUNK)
            s = dot_nt(kv_all[h, 0, rows, :], query)
            if c == NCHUNK - 1:
                s = s + bias[...]
            s_scr[rows, :] = s
            part = jnp.max(s.reshape(CHUNK // 8, 8, CHUNK), axis=0)
            top = part if top is None else jnp.maximum(top, part)
        top = jnp.max(top, axis=0, keepdims=True) * SCALE2
        total = jnp.zeros((8, CHUNK), F32)
        for c in range(NCHUNK):
            rows = slice(c * CHUNK, (c + 1) * CHUNK)
            p = jnp.exp2(s_scr[rows, :] * SCALE2 - top)
            total += jnp.sum(p.reshape(CHUNK // 8, 8, CHUNK), axis=0)
            p_scr[h, rows, cols] = p.astype(BF)
        total = jnp.sum(total, axis=0, keepdims=True)
        o = dot_nn(vt[h], p_scr[h, :, cols])
        for i in range(2):
            half = slice(i * ROWS, (i + 1) * ROWS)
            slot = 2 * pair + i
            o_part[h, slot] = o[:, half].astype(BF)
            st[h, slot, 0:1, :] = top[:, half]
            st[h, slot, 1:2, :] = total[:, half]

    INBOX = {("mid", 3): 0, ("mid", -3): 1, ("mid", 4): 2, 1: 3, -1: 4, 2: 5, -2: 6}

    def s_send(tag, h, srcs, boxes, key, to):
        i = INBOX[key]
        for n, (src, box) in enumerate(zip(srcs, boxes)):
            send(src, box.at[h, i], (tag, n, h, i), to_ctx=at_z(to))

    def s_recv(tag, h, boxes, key):
        i = INBOX[key]
        for n, box in enumerate(boxes):
            recv(box.at[h, i], (tag, n, h, i))
        return i

    def s_first(tag, h, parts, boxes):
        def at(off):
            return [p.at[h, SLOT[off]] for p in parts]

        s_send(tag, h, at(4), boxes, ("mid", 4), 2)
        s_send(tag, h, at(3), boxes, ("mid", 3), 1)
        s_send(tag, h, at(-3), boxes, ("mid", -3), -1)

    def s_near(tag, h, parts, boxes):
        for off in (1, -1):
            s_send(tag, h, [p.at[h, SLOT[off]] for p in parts], boxes, -off, off)

    o_parts, o_boxes = (o_part, st), (o_in, st_in)

    def merge(terms):
        peak = functools.reduce(jnp.maximum, [t[0] for t in terms])
        scales = [jnp.exp2(t[0] - peak) for t in terms]
        whole = sum(w * t[1] for w, t in zip(scales, terms))
        product = sum(w * t[2] for w, t in zip(scales, terms))
        return peak, whole, product

    def o_triple(h, slot):
        return st[h, slot, 0:1, :], st[h, slot, 1:2, :], o_part[h, slot].astype(F32)

    def o_arrived(h, key):
        i = s_recv("o", h, o_boxes, key)
        return st_in[h, i, 0:1, :], st_in[h, i, 1:2, :], o_in[h, i].astype(F32)

    def o_second(h):
        for n, off in enumerate((2, -2)):
            terms = [o_triple(h, SLOT[off]), o_arrived(h, ("mid", 3 if off > 0 else -3))]
            if off > 0:
                terms.append(o_arrived(h, ("mid", 4)))
            peak, whole, product = merge(terms)
            st_mid[h, n, 0:1, :] = peak
            st_mid[h, n, 1:2, :] = whole
            o_mid[h, n] = product.astype(BF)
            s_send("o", h, (o_mid.at[h, n], st_mid.at[h, n]), o_boxes, -off, off)

    attn = []

    def o_finish(h):
        terms = [o_triple(h, 0)] + [o_arrived(h, key) for key in (1, -1, 2, -2)]
        peak, whole, product = merge(terms)
        mine = (product / whole).T.astype(BF)
        attn.append(mine)
        both = mine.astype(F32) * do_all[h, 0:ROWS, :].astype(F32)
        delta = jnp.sum(both.T, axis=0, keepdims=True)
        ret[h, 0:1, :] = peak + jnp.log2(whole)
        ret[h, 1:2, :] = delta
        for off in OFFS[1:]:
            there = SLOT[-off]
            send(ret.at[h], ret_recv.at[h, there], ("ret", h, there), to_ctx=at_z(off))

    def settle(h):
        for slot in (0, 1, 2, 3, 4, 5, 6, 7):
            if slot:
                recv(ret_recv.at[h, slot], ("ret", h, slot))
            back = ret[h] if slot == 0 else ret_recv[h, slot]
            factor = jnp.exp2(st[h, slot, 0:1, :] - back[0:1])
            cd[h, 0:1, slot * ROWS : (slot + 1) * ROWS] = factor * back[1:2]
            rows = slice(slot * ROWS, (slot + 1) * ROWS)
            column = jnp.broadcast_to(factor, (ROWS, ROWS)).T
            dop[h, rows, :] = (do_all[h, rows, :].astype(F32) * column).astype(BF)

    def scores_back(h, chunks):
        for c in chunks:
            rows = slice(c * CHUNK, (c + 1) * CHUNK)
            value = kv_all[h, 1, rows, :]
            for pair in range(4):
                cols = slice(pair * CHUNK, (pair + 1) * CHUNK)
                dp = dot_nt(value, dop[h, cols, :])
                ds = p_scr[h, rows, cols].astype(F32) * (dp - cd[h, 0:1, cols])
                ds_scr[rows, cols] = ds.astype(BF)

    def keys_back(h, chunks):
        for c in chunks:
            rows = slice(c * CHUNK, (c + 1) * CHUNK)
            dkv_scr[h, rows, 0:HDIM] = dot_nn(ds_scr[rows, :], q_all[h]).astype(BF)
            dkv_scr[h, rows, HDIM : 2 * HDIM] = dot_nn(p_scr[h, rows, :], dop[h]).astype(BF)

    def queries_back(h):
        for pair in (3, 2, 1, 0):
            cols = slice(pair * CHUNK, (pair + 1) * CHUNK)
            dq = dot_nn(kt[h], ds_scr[:, cols])
            for i in range(2):
                dq_part[h, 2 * pair + i] = dq[:, i * ROWS : (i + 1) * ROWS].astype(BF)

    def dq_second(h):
        for n, off in enumerate((2, -2)):
            keys = [("mid", 3), ("mid", 4)] if off > 0 else [("mid", -3)]
            total = dq_part[h, SLOT[off]].astype(F32)
            for key in keys:
                total += dq_in[h, s_recv("dq", h, (dq_in,), key)].astype(F32)
            dq_mid[h, n] = total.astype(BF)
            s_send("dq", h, (dq_mid.at[h, n],), (dq_in,), -off, off)

    def dq_write(h, boxes):
        total = dq_part[h, 0].astype(F32)
        for i in boxes:
            total += dq_in[h, i].astype(F32)
        gq_ref[:, h * HDIM : (h + 1) * HDIM] = (total * SCALE).T.astype(BF)

    def dq_finish(h):
        dq_write(h, [s_recv("dq", h, (dq_in,), key) for key in (1, -1, 2, -2)])

    def dq_direct(h):
        for off in (4, 3, -3, 2, -2, 1, -1):
            i = SLOT[-off] - 1
            send(dq_part.at[h, SLOT[off]], dq_in.at[h, i], ("dq", 0, h, i), to_ctx=at_z(off))

    def dq_direct_finish(h):
        for i in range(NZ - 1):
            recv(dq_in.at[h, i], ("dq", 0, h, i))
        dq_write(h, range(NZ - 1))

    def keys_to_sibling(h):
        send(dkv_scr.at[h, pl.ds(SECT // 2, SECT // 2)], r1_sec.at[h], ("r1s", h), to_ctx=sibling)
        src = dkv_scr.at[h, pl.ds(SECT + HIST // 2, HIST // 2)]
        send(src, r1_hist.at[h], ("r1h", h), to_ctx=sibling)

    def keys_along_y(h):
        recv(r1_sec.at[h], ("r1s", h))
        recv(r1_hist.at[h], ("r1h", h))
        for dy in (2, 1, 3, 0):
            there = (NY - dy) % NY
            for name, got, total, into, start, size in (
                ("r2s", r1_sec, t_sec, r2_sec, 0, ROWS),
                ("r2h", r1_hist, t_hist, r2_hist, SECT, HCAP),
            ):
                rows = slice(dy * size, (dy + 1) * size)
                own = dkv_scr[h, start + dy * size : start + (dy + 1) * size, :].astype(F32)
                total[h, rows, :] = (own + got[h, rows, :].astype(F32)).astype(BF)
                if dy:
                    src = total.at[h, pl.ds(dy * size, size)]
                    send(src, into.at[h, there], (name, h, there), to_ctx=at_y(dy))

    def keys_finish(h):
        cols = slice(h * HDIM, (h + 1) * HDIM)
        for name, total, into, size, k_out, v_out in (
            ("r2s", t_sec, r2_sec, ROWS, gk_ref, gv_ref),
            ("r2h", t_hist, r2_hist, HCAP, ghk_ref, ghv_ref),
        ):
            value = total[h, 0:size, :].astype(F32)
            for dy in range(1, NY):
                recv(into.at[h, dy], (name, h, dy))
                value = value + into[h, dy].astype(F32)
            k_out[:, cols] = (value[:, 0:HDIM] * SCALE).astype(BF)
            v_out[:, cols] = value[:, HDIM : 2 * HDIM].astype(BF)

    def project():
        rows = jnp.concatenate(attn, axis=1)
        for dx in (2, 1, 3):
            there = (NX - dx) % NX
            po_send[dx] = dot_nn(rows, w_cols(dx)).astype(BF)
            send(po_send.at[dx], po_recv.at[there], ("po", there), to_head=at_x(dx))
        po_send[0] = dot_nn(rows, w_cols(0)).astype(BF)

    def project_finish():
        total = po_send[0].astype(F32)
        for dx in (1, 3, 2):
            recv(po_recv.at[dx], ("po", dx))
            total += po_recv[dx].astype(F32)
        out_ref[...] = total.astype(BF)

    o_first = functools.partial(s_first, "o", parts=o_parts, boxes=o_boxes)
    o_near = functools.partial(s_near, "o", parts=o_parts, boxes=o_boxes)
    dq_first = functools.partial(s_first, "dq", parts=(dq_part,), boxes=(dq_in,))
    dq_near = functools.partial(s_near, "dq", parts=(dq_part,), boxes=(dq_in,))

    z_second(q_all, "q", 0)
    kv_second(0)
    z_second(q_all, "q", 1)
    z_second(q_all, "q", 2)
    kv_rest(0)
    z_rest(q_all, "q", 0)
    forward(0, 3)
    forward(0, 2)
    o_first(0)
    kv_second(1)
    forward(0, 1)
    forward(0, 0)
    o_near(0)
    kv_second(2)
    cotangent()
    kv_rest(1)
    z_rest(q_all, "q", 1)
    forward(1, 3)
    forward(1, 2)
    o_first(1)
    o_second(0)
    forward(1, 1)
    z_second(do_all, "d", 0)
    forward(1, 0)
    o_near(1)
    z_second(do_all, "d", 1)
    kv_rest(2)
    z_rest(q_all, "q", 2)
    forward(2, 3)
    z_second(do_all, "d", 2)
    forward(2, 2)
    o_first(2)
    o_second(1)
    o_finish(0)
    forward(2, 1)
    forward(2, 0)
    o_near(2)
    z_rest(do_all, "d", 0)
    o_second(2)
    o_finish(1)
    settle(0)
    scores_back(0, (2, 3, 4))
    keys_back(0, (2, 3, 4))
    keys_to_sibling(0)
    o_finish(2)
    project()
    scores_back(0, (0, 1))
    queries_back(0)
    dq_first(0)
    dq_near(0)
    keys_back(0, (0, 1))
    z_rest(do_all, "d", 1)
    settle(1)
    keys_along_y(0)
    scores_back(1, (2, 3, 4))
    keys_back(1, (2, 3, 4))
    keys_to_sibling(1)
    dq_second(0)
    scores_back(1, (0, 1))
    queries_back(1)
    dq_first(1)
    dq_near(1)
    keys_back(1, (0, 1))
    z_rest(do_all, "d", 2)
    settle(2)
    keys_along_y(1)
    scores_back(2, (2, 3, 4))
    keys_back(2, (2, 3, 4))
    keys_to_sibling(2)
    dq_second(1)
    scores_back(2, (0, 1))
    queries_back(2)
    dq_direct(2)
    keys_back(2, (0, 1))
    keys_along_y(2)
    keys_finish(0)
    dq_finish(0)
    project_finish()
    keys_finish(1)
    dq_finish(1)
    keys_finish(2)
    dq_direct_finish(2)

    for copy in sent:
        copy.wait_send()
    assert len(sems.names) <= N_SEMS, len(sems.names)


def write_kernel(*refs):
    n = (len(refs) - 1) // 2
    sems = refs[-1]
    copies = [pltpu.make_async_copy(refs[i], refs[n + i], sems.at[i]) for i in range(n)]
    for copy in copies:
        copy.start()
    for copy in copies:
        copy.wait()


def write(arrays):
    n = len(arrays)
    return pl.pallas_call(
        write_kernel,
        out_shape=[jax.ShapeDtypeStruct(a.shape, a.dtype) for a in arrays],
        in_specs=[pl.BlockSpec(memory_space=pltpu.VMEM)] * n,
        out_specs=[pl.BlockSpec(memory_space=pl.ANY)] * n,
        scratch_shapes=[pltpu.SemaphoreType.DMA((n,))],
    )(*arrays)


def shards(sec_q, sec_k, sec_v, hist_k, hist_v, frame_levels, frame_counts, w_out, grad_out):
    vmem = pl.BlockSpec(memory_space=pltpu.VMEM)
    smem = pl.BlockSpec(memory_space=pltpu.SMEM)
    anywhere = pl.BlockSpec(memory_space=pl.ANY)
    box = (HEADS, NZ, HDIM, ROWS)
    mid = (HEADS, 2, HDIM, ROWS)
    scratch = [
        pltpu.VMEM((HEADS, QT, HDIM), BF),
        pltpu.VMEM((HEADS, 2, KT, HDIM), BF),
        pltpu.VMEM((HEADS, HDIM, KT), BF),
        pltpu.VMEM((HEADS, HDIM, KT), BF),
        pltpu.VMEM((WIDTH, NX * OCOLS), BF),
        pltpu.VMEM((NX, ROWS, OCOLS), BF),
        pltpu.VMEM((HEADS, QT, HDIM), BF),
        pltpu.VMEM((HEADS, QT, HDIM), BF),
        pltpu.VMEM((HIST, CHUNK), F32),
        pltpu.VMEM((KT, CHUNK), F32),
        pltpu.VMEM((HEADS, KT, QT), BF),
        pltpu.VMEM(box, BF),
        pltpu.VMEM((KT, QT), BF),
        pltpu.VMEM(box, BF),
        pltpu.VMEM((HEADS, KT, 2 * HDIM), BF),
        pltpu.VMEM((HEADS, NZ, 8, ROWS), F32),
        pltpu.VMEM((HEADS, 8, ROWS), F32),
        pltpu.VMEM((HEADS, NZ, 8, ROWS), F32),
        pltpu.VMEM((HEADS, 8, QT), F32),
        pltpu.VMEM(mid, BF),
        pltpu.VMEM(box, BF),
        pltpu.VMEM((HEADS, 2, 8, ROWS), F32),
        pltpu.VMEM((HEADS, NZ, 8, ROWS), F32),
        pltpu.VMEM(mid, BF),
        pltpu.VMEM(box, BF),
        pltpu.VMEM((HEADS, SECT // 2, 2 * HDIM), BF),
        pltpu.VMEM((HEADS, HIST // 2, 2 * HDIM), BF),
        pltpu.VMEM((HEADS, SECT // 2, 2 * HDIM), BF),
        pltpu.VMEM((HEADS, HIST // 2, 2 * HDIM), BF),
        pltpu.VMEM((HEADS, NY, ROWS, 2 * HDIM), BF),
        pltpu.VMEM((HEADS, NY, HCAP, 2 * HDIM), BF),
        pltpu.VMEM((NX, ROWS, OCOLS), BF),
        pltpu.VMEM((NX, ROWS, OCOLS), BF),
        pltpu.SemaphoreType.DMA((N_SEMS,)),
        pltpu.SemaphoreType.DMA((N_SEMS,)),
        pltpu.SemaphoreType.DMA(()),
    ]
    shapes = [
        jax.ShapeDtypeStruct((ROWS, OCOLS), BF),
        jax.ShapeDtypeStruct((ROWS, WIDTH), BF),
        jax.ShapeDtypeStruct((ROWS, WIDTH), BF),
        jax.ShapeDtypeStruct((ROWS, WIDTH), BF),
        jax.ShapeDtypeStruct((HCAP, WIDTH), BF),
        jax.ShapeDtypeStruct((HCAP, WIDTH), BF),
    ]
    results = pl.pallas_call(
        kernel,
        out_shape=shapes,
        in_specs=[vmem] * 5 + [smem] * 2 + [anywhere, vmem],
        out_specs=[vmem] * 6,
        scratch_shapes=scratch,
        compiler_params=pltpu.CompilerParams(
            collective_id=0, has_side_effects=True, vmem_limit_bytes=60 * 1024 * 1024
        ),
    )(sec_q, sec_k, sec_v, hist_k, hist_v, frame_levels.T, frame_counts, w_out, grad_out)
    return write(results)


def solution(mesh):
    both = P("ctx", "head")
    placed = (both, both, both, both, both, P(), P(), P("head", None), both)
    return jax.shard_map(
        shards, mesh=mesh, in_specs=placed, out_specs=(both,) * 6, check_vma=False
    )
```

```python
import functools
import math

import jax
import jax.numpy as jnp
from jax import lax
from jax.experimental import pallas as pl
from jax.experimental.pallas import tpu as pltpu
from jax.sharding import PartitionSpec as P

HDIM = 128
FTOK = 16
FMAX = 2
NEG_FILL = -1e30
MESH = pl.DeviceIdType.MESH

NZ, NY, NC, NX = 8, 4, 2, 4
HEADS = 3
ROWS = 128
HCAP = 32
QT = NZ * ROWS
SECT = NY * NC * ROWS
HIST = NY * NC * HCAP
KT = SECT + HIST
CHUNK = 256
NCHUNK = KT // CHUNK
WIDTH = HEADS * HDIM
OCOLS = 768
BF = jnp.bfloat16
F32 = jnp.float32

OFFS = (0, 1, -1, 2, -2, 3, -3, 4)
SLOT = {off: i for i, off in enumerate(OFFS)}
SLOT[-4] = SLOT[4]

DIRECT = {o: o for o in OFFS[1:]}
TWO = {4: 2, 3: 1, -3: -1, 2: 2, -2: -2, 1: 1, -1: -1}
THREE = {4: 2, 3: 1, -3: -1, 2: 1, -2: -1, 1: 1, -1: -1}
RING = {4: 1, 3: 1, -3: -1, 2: 1, -2: -1, 1: 1, -1: -1}


def feeders(route, off):
    return [o for o in OFFS[1:] if o - route[o] == off]


def depth(route, off):
    return 0 if off == 0 else 1 + depth(route, off - route[off])


def layer(route, n):
    return [o for o in OFFS if depth(route, o) == n]


SCALE = 1.0 / math.sqrt(HDIM)
SCALE2 = SCALE * math.log2(math.e)


def dot_nn(a, b):
    return lax.dot_general(a, b, (((1,), (0,)), ((), ())), preferred_element_type=F32)


def dot_nt(a, b):
    return lax.dot_general(a, b, (((1,), (1,)), ((), ())), preferred_element_type=F32)


class Sems:
    def __init__(self):
        self.names = {}

    def __call__(self, *name):
        return self.names.setdefault(name, len(self.names))


N_SEMS = 256
Q_ROUTE, D_ROUTE = TWO, THREE
O_ROUTE = (TWO, TWO, TWO)
DQ_ROUTE = (DIRECT, TWO, TWO)


def kernel(
    q_ref, k_ref, v_ref, hk_ref, hv_ref, lev_ref, cnt_ref, w_hbm, g_ref,
    out_ref, gq_ref, gk_ref, gv_ref, ghk_ref, ghv_ref,
    q_all, kv_all, kt, vt, w_all, g_all, do_all, dop, bias,
    s_scr, p_scr, o_part, ds_scr, dq_part, dkv_scr,
    st, ret, ret_recv, cd,
    o_mid, o_in, st_mid, st_in, dq_mid, dq_in,
    r1_sec, r1_hist, t_sec, t_hist, r2_sec, r2_hist,
    at_all, w_far, acc,
    send_sem, recv_sem, w_sem,
):
    ctx = lax.axis_index("ctx")
    x = lax.axis_index("head")
    core = lax.rem(ctx, NC)
    y = lax.rem(ctx // NC, NY)
    z = ctx // (NC * NY)
    way = 1 - 2 * core

    def at_z(off):
        return (lax.rem(z + off * way + 2 * NZ, NZ) * NY + y) * NC + core

    def at_y(dy):
        return (z * NY + lax.rem(y + dy, NY)) * NC + core

    def at_x(dx):
        return lax.rem(x + dx, NX)

    sibling = (z * NY + y) * NC + (1 - core)

    sems = Sems()
    sent = []

    def send(src, dst, name, to_ctx=None, to_head=None):
        i = sems(*name)
        copy = pltpu.make_async_remote_copy(
            src_ref=src, dst_ref=dst, send_sem=send_sem.at[i], recv_sem=recv_sem.at[i],
            device_id=(ctx if to_ctx is None else to_ctx, x if to_head is None else to_head),
            device_id_type=MESH,
        )
        copy.start()
        sent.append(copy)

    def recv(dst, name):
        i = sems(*name)
        pltpu.make_async_remote_copy(
            src_ref=dst, dst_ref=dst, send_sem=send_sem.at[i], recv_sem=recv_sem.at[i],
            device_id=(sibling, x), device_id_type=MESH,
        ).wait_recv()

    barrier = pltpu.get_barrier_semaphore()
    peers = [(at_z(o), x) for o in OFFS[1:]]
    peers += [(at_y(d), x) for d in range(1, NY)]
    peers += [(sibling, x)]
    peers += [(ctx, at_x(d)) for d in range(1, NX)]
    for peer in peers:
        pl.semaphore_signal(barrier, inc=1, device_id=peer, device_id_type=MESH)

    w_copy = pltpu.make_async_copy(w_hbm, w_all, w_sem)
    w_copy.start()
    for h in range(HEADS):
        cols = slice(h * HDIM, (h + 1) * HDIM)
        q_all[h, 0:ROWS, :] = q_ref[:, cols]
        kv_all[h, 0, 0:ROWS, :] = k_ref[:, cols]
        kv_all[h, 0, SECT : SECT + HCAP, :] = hk_ref[:, cols]
        kv_all[h, 1, 0:ROWS, :] = v_ref[:, cols]
        kv_all[h, 1, SECT : SECT + HCAP, :] = hv_ref[:, cols]

    pl.semaphore_wait(barrier, len(peers))

    def z_slot(buf, h, off):
        return buf.at[h, pl.ds(SLOT[off] * ROWS, ROWS), :]

    bufs = {"q": (q_all, Q_ROUTE), "d": (do_all, D_ROUTE)}

    def gather(tag, h, n):
        buf, route = bufs[tag]
        for o in layer(route, n):
            if not feeders(route, o):
                continue
            if o:
                recv(z_slot(buf, h, o), (tag, h, o))
            for off in feeders(route, o):
                dst = z_slot(buf, h, off)
                send(z_slot(buf, h, o), dst, (tag, h, off), to_ctx=at_z(-route[off]))

    def gather_rest(tag, h):
        buf, route = bufs[tag]
        for o in OFFS[1:]:
            if not feeders(route, o):
                recv(z_slot(buf, h, o), (tag, h, o))

    pieces = ((0, ROWS), (SECT, HCAP))

    def kv_first(h):
        for dy in (2, 1, 3):
            there = (NY - dy) % NY
            for start, size in pieces:
                src = kv_all.at[h, :, pl.ds(start, size), :]
                dst = kv_all.at[h, :, pl.ds(start + there * size, size), :]
                send(src, dst, ("kv", h, there, start), to_ctx=at_y(dy))

    def kv_second(h):
        for dy in (1, 3, 2):
            for start, size in pieces:
                recv(kv_all.at[h, :, pl.ds(start + dy * size, size), :], ("kv", h, dy, start))
        for start, size in pieces:
            src = kv_all.at[h, :, pl.ds(start, NY * size), :]
            dst = kv_all.at[h, :, pl.ds(start + NY * size, NY * size), :]
            send(src, dst, ("kv", h, "sib", start), to_ctx=sibling)

    def kv_rest(h):
        for start, size in pieces:
            dst = kv_all.at[h, :, pl.ds(start + NY * size, NY * size), :]
            recv(dst, ("kv", h, "sib", start))
        for i in range(KT // HDIM):
            rows = slice(i * HDIM, (i + 1) * HDIM)
            kt[h, :, rows] = kv_all[h, 0, rows, :].T
            vt[h, :, rows] = kv_all[h, 1, rows, :].T

    for dx in (2, 1, 3):
        there = (NX - dx) % NX
        send(g_ref, g_all.at[there], ("g", there), to_head=at_x(dx))
    for h in range(HEADS):
        kv_first(h)
        gather("q", h, 0)

    row = lax.broadcasted_iota(jnp.int32, (HIST, CHUNK), 0)
    limit = jnp.zeros((HIST, CHUNK), jnp.int32)
    for dc in range(NC):
        for dy in range(NY):
            owner = (z * NY + lax.rem(y + dy, NY)) * NC + (core if dc == 0 else 1 - core)
            tokens = jnp.int32(0)
            for f in range(FMAX):
                level = lev_ref[f, owner]
                size = lax.shift_right_logical(jnp.int32(FTOK), 2 * level)
                tokens = tokens + jnp.where(f < cnt_ref[owner], size, 0)
            j = dc * NY + dy
            mine = (row >= j * HCAP) & (row < (j + 1) * HCAP)
            limit = jnp.where(mine, tokens + j * HCAP, limit)
    bias[...] = jnp.where(row < limit, 0.0, NEG_FILL)

    def w_cols(dx):
        return w_all[:, pl.ds(pl.multiple_of(at_x(dx) * OCOLS, OCOLS), OCOLS)]

    def cotangent():
        w_copy.wait()
        d_attn = dot_nt(g_ref[...], w_cols(0))
        for dx in (1, 3, 2):
            recv(g_all.at[dx], ("g", dx))
            d_attn += dot_nt(g_all[dx], w_cols(dx))
        for h in range(HEADS):
            do_all[h, 0:ROWS, :] = d_attn[:, h * HDIM : (h + 1) * HDIM].astype(BF)

    def forward(h, pair):
        cols = slice(pair * CHUNK, (pair + 1) * CHUNK)
        query = q_all[h, cols, :]
        top = None
        for c in range(NCHUNK):
            rows = slice(c * CHUNK, (c + 1) * CHUNK)
            s = dot_nt(kv_all[h, 0, rows, :], query)
            if c == NCHUNK - 1:
                s = s + bias[...]
            s_scr[rows, :] = s
            part = jnp.max(s.reshape(CHUNK // 8, 8, CHUNK), axis=0)
            top = part if top is None else jnp.maximum(top, part)
        top = jnp.max(top, axis=0, keepdims=True) * SCALE2
        total = jnp.zeros((8, CHUNK), F32)
        for c in range(NCHUNK):
            rows = slice(c * CHUNK, (c + 1) * CHUNK)
            p = jnp.exp2(s_scr[rows, :] * SCALE2 - top)
            total += jnp.sum(p.reshape(CHUNK // 8, 8, CHUNK), axis=0)
            p_scr[h, rows, cols] = p.astype(BF)
        total = jnp.sum(total, axis=0, keepdims=True)
        o = dot_nn(vt[h], p_scr[h, :, cols])
        for i in range(2):
            half = slice(i * ROWS, (i + 1) * ROWS)
            slot = 2 * pair + i
            o_part[h, slot] = o[:, half].astype(BF)
            st[h, slot, 0:1, :] = top[:, half]
            st[h, slot, 1:2, :] = total[:, half]

    def s_send(tag, h, off, srcs, boxes, route):
        i = SLOT[off] - 1
        for n, (src, box) in enumerate(zip(srcs, boxes)):
            send(src, box.at[h, i], (tag, n, h, i), to_ctx=at_z(route[off]))

    def s_recv(tag, h, off, boxes):
        i = SLOT[off] - 1
        for n, box in enumerate(boxes):
            recv(box.at[h, i], (tag, n, h, i))
        return i

    def stage(route, n):
        return layer(route, max(depth(route, o) for o in OFFS) + 1 - n)

    def merge(terms):
        peak = functools.reduce(jnp.maximum, [t[0] for t in terms])
        scales = [jnp.exp2(t[0] - peak) for t in terms]
        whole = sum(w * t[1] for w, t in zip(scales, terms))
        product = sum(w * t[2] for w, t in zip(scales, terms))
        return peak, whole, product

    def o_triple(h, slot):
        return st[h, slot, 0:1, :], st[h, slot, 1:2, :], o_part[h, slot].astype(F32)

    def o_arrived(h, off):
        i = s_recv("o", h, off, (o_in, st_in))
        return st_in[h, i, 0:1, :], st_in[h, i, 1:2, :], o_in[h, i].astype(F32)

    def o_stage(h, n):
        route = O_ROUTE[h]
        for off in stage(route, n):
            slot = SLOT[off]
            srcs = (o_part.at[h, slot], st.at[h, slot])
            before = feeders(route, off)
            if before:
                terms = [o_triple(h, slot)] + [o_arrived(h, o) for o in before]
                peak, whole, product = merge(terms)
                st_mid[h, slot, 0:1, :] = peak
                st_mid[h, slot, 1:2, :] = whole
                o_mid[h, slot] = product.astype(BF)
                srcs = (o_mid.at[h, slot], st_mid.at[h, slot])
            s_send("o", h, off, srcs, (o_in, st_in), route)

    def o_finish(h):
        terms = [o_triple(h, 0)] + [o_arrived(h, o) for o in feeders(O_ROUTE[h], 0)]
        peak, whole, product = merge(terms)
        mine = (product / whole).T.astype(BF)
        at_all[h, 0] = mine
        for dx in (2, 1, 3):
            there = (NX - dx) % NX
            send(at_all.at[h, 0], at_all.at[h, there], ("at", h, there), to_head=at_x(dx))
        both = mine.astype(F32) * do_all[h, 0:ROWS, :].astype(F32)
        delta = jnp.sum(both.T, axis=0, keepdims=True)
        ret[h, 0:1, :] = peak + jnp.log2(whole)
        ret[h, 1:2, :] = delta
        for off in OFFS[1:]:
            there = SLOT[-off]
            send(ret.at[h], ret_recv.at[h, there], ("ret", h, there), to_ctx=at_z(off))

    def settle(h):
        for slot in (0, 1, 2, 3, 4, 5, 6, 7):
            if slot:
                recv(ret_recv.at[h, slot], ("ret", h, slot))
            back = ret[h] if slot == 0 else ret_recv[h, slot]
            factor = jnp.exp2(st[h, slot, 0:1, :] - back[0:1])
            cd[h, 0:1, slot * ROWS : (slot + 1) * ROWS] = factor * back[1:2]
            rows = slice(slot * ROWS, (slot + 1) * ROWS)
            column = jnp.broadcast_to(factor, (ROWS, ROWS)).T
            dop[h, rows, :] = (do_all[h, rows, :].astype(F32) * column).astype(BF)

    def scores_back(h, chunks):
        for c in chunks:
            rows = slice(c * CHUNK, (c + 1) * CHUNK)
            value = kv_all[h, 1, rows, :]
            for pair in range(4):
                cols = slice(pair * CHUNK, (pair + 1) * CHUNK)
                dp = dot_nt(value, dop[h, cols, :])
                ds = p_scr[h, rows, cols].astype(F32) * (dp - cd[h, 0:1, cols])
                ds_scr[rows, cols] = ds.astype(BF)

    def keys_back(h, chunks):
        for c in chunks:
            rows = slice(c * CHUNK, (c + 1) * CHUNK)
            dkv_scr[h, rows, 0:HDIM] = dot_nn(ds_scr[rows, :], q_all[h]).astype(BF)
            dkv_scr[h, rows, HDIM : 2 * HDIM] = dot_nn(p_scr[h, rows, :], dop[h]).astype(BF)

    def queries_back(h):
        for pair in (3, 2, 1, 0):
            cols = slice(pair * CHUNK, (pair + 1) * CHUNK)
            dq = dot_nn(kt[h], ds_scr[:, cols])
            for i in range(2):
                dq_part[h, 2 * pair + i] = dq[:, i * ROWS : (i + 1) * ROWS].astype(BF)

    def dq_stage(h, n):
        route = DQ_ROUTE[h]
        for off in stage(route, n):
            slot = SLOT[off]
            src = dq_part.at[h, slot]
            before = feeders(route, off)
            if before:
                total = dq_part[h, slot].astype(F32)
                for o in before:
                    total += dq_in[h, s_recv("dq", h, o, (dq_in,))].astype(F32)
                dq_mid[h, slot] = total.astype(BF)
                src = dq_mid.at[h, slot]
            s_send("dq", h, off, (src,), (dq_in,), route)

    def dq_finish(h):
        total = dq_part[h, 0].astype(F32)
        for o in feeders(DQ_ROUTE[h], 0):
            total += dq_in[h, s_recv("dq", h, o, (dq_in,))].astype(F32)
        gq_ref[:, h * HDIM : (h + 1) * HDIM] = (total * SCALE).T.astype(BF)

    def keys_to_sibling(h):
        send(dkv_scr.at[h, pl.ds(SECT // 2, SECT // 2)], r1_sec.at[h], ("r1s", h), to_ctx=sibling)
        src = dkv_scr.at[h, pl.ds(SECT + HIST // 2, HIST // 2)]
        send(src, r1_hist.at[h], ("r1h", h), to_ctx=sibling)

    def keys_along_y(h):
        recv(r1_sec.at[h], ("r1s", h))
        recv(r1_hist.at[h], ("r1h", h))
        for dy in (2, 1, 3, 0):
            there = (NY - dy) % NY
            for name, got, total, into, start, size in (
                ("r2s", r1_sec, t_sec, r2_sec, 0, ROWS),
                ("r2h", r1_hist, t_hist, r2_hist, SECT, HCAP),
            ):
                rows = slice(dy * size, (dy + 1) * size)
                own = dkv_scr[h, start + dy * size : start + (dy + 1) * size, :].astype(F32)
                total[h, rows, :] = (own + got[h, rows, :].astype(F32)).astype(BF)
                if dy:
                    src = total.at[h, pl.ds(dy * size, size)]
                    send(src, into.at[h, there], (name, h, there), to_ctx=at_y(dy))

    def keys_finish(h):
        cols = slice(h * HDIM, (h + 1) * HDIM)
        for name, total, into, size, k_out, v_out in (
            ("r2s", t_sec, r2_sec, ROWS, gk_ref, gv_ref),
            ("r2h", t_hist, r2_hist, HCAP, ghk_ref, ghv_ref),
        ):
            value = total[h, 0:size, :].astype(F32)
            for dy in range(1, NY):
                recv(into.at[h, dy], (name, h, dy))
                value = value + into[h, dy].astype(F32)
            k_out[:, cols] = (value[:, 0:HDIM] * SCALE).astype(BF)
            v_out[:, cols] = value[:, HDIM : 2 * HDIM].astype(BF)

    def half(base):
        return pl.ds(pl.multiple_of(base + core * (OCOLS // 2), OCOLS // 2), OCOLS // 2)

    def w_first():
        for dx in (2, 1, 3):
            there = (NX - dx) % NX
            src = w_all.at[:, half(at_x(dx) * OCOLS)]
            send(src, w_far.at[there, :, half(0)], ("w", there), to_head=at_x(dx))

    def w_second():
        for dx in (1, 3, 2):
            recv(w_far.at[dx, :, half(0)], ("w", dx))
            send(w_far.at[dx, :, half(0)], w_far.at[dx, :, half(0)], ("ws", dx), to_ctx=sibling)

    def w_rest():
        for dx in (1, 3, 2):
            recv(w_far.at[dx, :, half(0)], ("ws", dx))

    def project(heads, first, last):
        rows = slice(heads[0] * HDIM, (heads[-1] + 1) * HDIM)
        total = None if first else acc[...]
        for dx in (0, 1, 3, 2):
            if dx:
                for h in heads:
                    recv(at_all.at[h, dx], ("at", h, dx))
            left = jnp.concatenate([at_all[h, dx] for h in heads], axis=1)
            part = dot_nn(left, w_far[dx, rows, :] if dx else w_cols(0)[rows, :])
            total = part if total is None else total + part
        if last:
            out_ref[...] = total.astype(BF)
        else:
            acc[...] = total

    gather("q", 0, 1)
    kv_second(0)
    gather("q", 1, 1)
    gather("q", 2, 1)
    kv_rest(0)
    kv_second(1)
    gather_rest("q", 0)
    forward(0, 2)
    cotangent()
    gather("d", 0, 0)
    gather("d", 1, 0)
    forward(0, 3)
    kv_second(2)
    kv_rest(1)
    o_stage(0, 1)
    gather_rest("q", 1)
    forward(1, 2)
    gather("d", 2, 0)
    forward(1, 3)
    gather_rest("q", 2)
    kv_rest(2)
    gather("d", 0, 1)
    o_stage(1, 1)
    w_first()
    forward(0, 1)
    forward(0, 0)
    o_stage(0, 2)
    gather("d", 1, 1)
    forward(1, 1)
    forward(2, 3)
    gather("d", 2, 1)
    forward(2, 2)
    gather("d", 0, 2)
    o_stage(2, 1)
    forward(2, 0)
    forward(2, 1)
    forward(1, 0)
    o_finish(0)
    o_stage(1, 2)
    o_stage(2, 2)
    gather("d", 1, 2)
    gather_rest("d", 0)
    settle(0)
    scores_back(0, (0, 1))
    o_finish(1)
    gather("d", 2, 2)
    scores_back(0, (2, 3, 4))
    keys_back(0, (2, 3, 4))
    keys_to_sibling(0)
    o_finish(2)
    queries_back(0)
    dq_stage(0, 1)
    w_second()
    keys_back(0, (0, 1))
    gather_rest("d", 1)
    keys_along_y(0)
    settle(1)
    scores_back(1, (0, 1))
    keys_back(1, (0, 1))
    scores_back(1, (2, 3, 4))
    keys_back(1, (2, 3, 4))
    gather_rest("d", 2)
    queries_back(1)
    keys_to_sibling(1)
    dq_stage(1, 1)
    settle(2)
    scores_back(2, (0, 1))
    scores_back(2, (2, 3, 4))
    keys_along_y(1)
    queries_back(2)
    dq_stage(2, 1)
    keys_back(2, (2, 3, 4))
    keys_to_sibling(2)
    keys_back(2, (0, 1))
    dq_stage(1, 2)
    keys_along_y(2)
    dq_stage(2, 2)
    w_rest()
    dq_finish(0)
    keys_finish(1)
    project((0, 1), True, False)
    keys_finish(0)
    project((2,), False, True)
    dq_finish(1)
    keys_finish(2)
    dq_finish(2)

    for copy in sent:
        copy.wait_send()
    assert len(sems.names) <= N_SEMS, len(sems.names)


def write_kernel(*refs):
    n = (len(refs) - 1) // 2
    sems = refs[-1]
    copies = [pltpu.make_async_copy(refs[i], refs[n + i], sems.at[i]) for i in range(n)]
    for copy in copies:
        copy.start()
    for copy in copies:
        copy.wait()


def write(arrays):
    n = len(arrays)
    return pl.pallas_call(
        write_kernel,
        out_shape=[jax.ShapeDtypeStruct(a.shape, a.dtype) for a in arrays],
        in_specs=[pl.BlockSpec(memory_space=pltpu.VMEM)] * n,
        out_specs=[pl.BlockSpec(memory_space=pl.ANY)] * n,
        scratch_shapes=[pltpu.SemaphoreType.DMA((n,))],
    )(*arrays)


def shards(sec_q, sec_k, sec_v, hist_k, hist_v, frame_levels, frame_counts, w_out, grad_out):
    vmem = pl.BlockSpec(memory_space=pltpu.VMEM)
    smem = pl.BlockSpec(memory_space=pltpu.SMEM)
    anywhere = pl.BlockSpec(memory_space=pl.ANY)
    box = (HEADS, NZ, HDIM, ROWS)
    scratch = [
        pltpu.VMEM((HEADS, QT, HDIM), BF),
        pltpu.VMEM((HEADS, 2, KT, HDIM), BF),
        pltpu.VMEM((HEADS, HDIM, KT), BF),
        pltpu.VMEM((HEADS, HDIM, KT), BF),
        pltpu.VMEM((WIDTH, NX * OCOLS), BF),
        pltpu.VMEM((NX, ROWS, OCOLS), BF),
        pltpu.VMEM((HEADS, QT, HDIM), BF),
        pltpu.VMEM((HEADS, QT, HDIM), BF),
        pltpu.VMEM((HIST, CHUNK), F32),
        pltpu.VMEM((KT, CHUNK), F32),
        pltpu.VMEM((HEADS, KT, QT), BF),
        pltpu.VMEM(box, BF),
        pltpu.VMEM((KT, QT), BF),
        pltpu.VMEM(box, BF),
        pltpu.VMEM((HEADS, KT, 2 * HDIM), BF),
        pltpu.VMEM((HEADS, NZ, 2, ROWS), F32),
        pltpu.VMEM((HEADS, 2, ROWS), F32),
        pltpu.VMEM((HEADS, NZ, 2, ROWS), F32),
        pltpu.VMEM((HEADS, 8, QT), F32),
        pltpu.VMEM(box, BF),
        pltpu.VMEM(box, BF),
        pltpu.VMEM((HEADS, NZ, 2, ROWS), F32),
        pltpu.VMEM((HEADS, NZ, 2, ROWS), F32),
        pltpu.VMEM(box, BF),
        pltpu.VMEM(box, BF),
        pltpu.VMEM((HEADS, SECT // 2, 2 * HDIM), BF),
        pltpu.VMEM((HEADS, HIST // 2, 2 * HDIM), BF),
        pltpu.VMEM((HEADS, SECT // 2, 2 * HDIM), BF),
        pltpu.VMEM((HEADS, HIST // 2, 2 * HDIM), BF),
        pltpu.VMEM((HEADS, NY, ROWS, 2 * HDIM), BF),
        pltpu.VMEM((HEADS, NY, HCAP, 2 * HDIM), BF),
        pltpu.VMEM((HEADS, NX, ROWS, HDIM), BF),
        pltpu.VMEM((NX, WIDTH, OCOLS), BF),
        pltpu.VMEM((ROWS, OCOLS), F32),
        pltpu.SemaphoreType.DMA((N_SEMS,)),
        pltpu.SemaphoreType.DMA((N_SEMS,)),
        pltpu.SemaphoreType.DMA(()),
    ]
    shapes = [
        jax.ShapeDtypeStruct((ROWS, OCOLS), BF),
        jax.ShapeDtypeStruct((ROWS, WIDTH), BF),
        jax.ShapeDtypeStruct((ROWS, WIDTH), BF),
        jax.ShapeDtypeStruct((ROWS, WIDTH), BF),
        jax.ShapeDtypeStruct((HCAP, WIDTH), BF),
        jax.ShapeDtypeStruct((HCAP, WIDTH), BF),
    ]
    results = pl.pallas_call(
        kernel,
        out_shape=shapes,
        in_specs=[vmem] * 5 + [smem] * 2 + [anywhere, vmem],
        out_specs=[vmem] * 6,
        scratch_shapes=scratch,
        compiler_params=pltpu.CompilerParams(
            collective_id=0, has_side_effects=True, vmem_limit_bytes=60 * 1024 * 1024
        ),
    )(sec_q, sec_k, sec_v, hist_k, hist_v, frame_levels.T, frame_counts, w_out, grad_out)
    return write(results)


def solution(mesh):
    both = P("ctx", "head")
    placed = (both, both, both, both, both, P(), P(), P("head", None), both)
    return jax.shard_map(
        shards, mesh=mesh, in_specs=placed, out_specs=(both,) * 6, check_vma=False
    )
```

```python
import functools
import math

import jax
import jax.numpy as jnp
from jax import lax
from jax.experimental import pallas as pl
from jax.experimental.pallas import tpu as pltpu
from jax.sharding import PartitionSpec as P

HDIM = 128
FTOK = 16
FMAX = 2
NEG_FILL = -1e30
MESH = pl.DeviceIdType.MESH

NZ, NY, NC, NX = 8, 4, 2, 4
HEADS = 3
ROWS = 128
HCAP = 32
QT = NZ * ROWS
SECT = NY * NC * ROWS
HIST = NY * NC * HCAP
KT = SECT + HIST
CHUNK = 256
NCHUNK = KT // CHUNK
WIDTH = HEADS * HDIM
OCOLS = 768
BF = jnp.bfloat16
F32 = jnp.float32

OFFS = (0, 1, -1, 2, -2, 3, -3, 4)
SLOT = {off: i for i, off in enumerate(OFFS)}
SLOT[-4] = SLOT[4]

DIRECT = {o: o for o in OFFS[1:]}
TWO = {4: 2, 3: 1, -3: -1, 2: 2, -2: -2, 1: 1, -1: -1}
THREE = {4: 2, 3: 1, -3: -1, 2: 1, -2: -1, 1: 1, -1: -1}
RING = {4: 1, 3: 1, -3: -1, 2: 1, -2: -1, 1: 1, -1: -1}


def feeders(route, off):
    return [o for o in OFFS[1:] if o - route[o] == off]


def depth(route, off):
    return 0 if off == 0 else 1 + depth(route, off - route[off])


def layer(route, n):
    return [o for o in OFFS if depth(route, o) == n]


SCALE = 1.0 / math.sqrt(HDIM)
SCALE2 = SCALE * math.log2(math.e)


def dot_nn(a, b):
    return lax.dot_general(a, b, (((1,), (0,)), ((), ())), preferred_element_type=F32)


def dot_nt(a, b):
    return lax.dot_general(a, b, (((1,), (1,)), ((), ())), preferred_element_type=F32)


class Sems:
    def __init__(self):
        self.names = {}

    def __call__(self, *name):
        return self.names.setdefault(name, len(self.names))


N_SEND, N_RECV = 16, 88
Q_ROUTE, D_ROUTE = TWO, THREE
O_ROUTE = (TWO, TWO, TWO)
DQ_ROUTE = (DIRECT, TWO, TWO)


def kernel(
    q_ref, k_ref, v_ref, hk_ref, hv_ref, lev_ref, cnt_ref, w_hbm, g_ref,
    out_ref, gq_ref, gk_ref, gv_ref, ghk_ref, ghv_ref,
    q_all, kv_all, kt, vt, w_all, g_all, do_all, dop, bias,
    s_scr, p_scr, o_part, ds_scr, dq_part, dkv_scr,
    st, ret, ret_recv, cd,
    o_mid, o_in, st_mid, st_in, dq_mid, dq_in,
    r1_sec, r1_hist, t_sec, t_hist, r2_sec, r2_hist,
    at_all, w_far, acc,
    send_sem, recv_sem, w_sem,
):
    ctx = lax.axis_index("ctx")
    x = lax.axis_index("head")
    core = lax.rem(ctx, NC)
    y = lax.rem(ctx // NC, NY)
    z = ctx // (NC * NY)
    way = 1 - 2 * core

    def at_z(off):
        return (lax.rem(z + off * way + 2 * NZ, NZ) * NY + y) * NC + core

    def at_y(dy):
        return (z * NY + lax.rem(y + dy, NY)) * NC + core

    def at_x(dx):
        return lax.rem(x + dx, NX)

    sibling = (z * NY + y) * NC + (1 - core)

    groups, arrivals = Sems(), Sems()

    def remote(src, dst, group, key, to_ctx, to_head):
        return pltpu.make_async_remote_copy(
            src_ref=src, dst_ref=dst,
            send_sem=send_sem.at[groups(group)], recv_sem=recv_sem.at[arrivals(*key)],
            device_id=(ctx if to_ctx is None else to_ctx, x if to_head is None else to_head),
            device_id_type=MESH,
        )

    def send(src, dst, group, key, to_ctx=None, to_head=None):
        remote(src, dst, group, key, to_ctx, to_head).start()

    def recv(same_size, group, key):
        remote(same_size, same_size, group, key, sibling, None).wait_recv()

    barrier = pltpu.get_barrier_semaphore()
    peers = [(at_z(o), x) for o in OFFS[1:]]
    peers += [(at_y(d), x) for d in range(1, NY)]
    peers += [(sibling, x)]
    peers += [(ctx, at_x(d)) for d in range(1, NX)]
    for peer in peers:
        pl.semaphore_signal(barrier, inc=1, device_id=peer, device_id_type=MESH)

    w_copy = pltpu.make_async_copy(w_hbm, w_all, w_sem)
    w_copy.start()
    for h in range(HEADS):
        cols = slice(h * HDIM, (h + 1) * HDIM)
        q_all[h, 0:ROWS, :] = q_ref[:, cols]
        kv_all[h, 0, 0:ROWS, :] = k_ref[:, cols]
        kv_all[h, 0, SECT : SECT + HCAP, :] = hk_ref[:, cols]
        kv_all[h, 1, 0:ROWS, :] = v_ref[:, cols]
        kv_all[h, 1, SECT : SECT + HCAP, :] = hv_ref[:, cols]

    pl.semaphore_wait(barrier, len(peers))

    def z_slot(buf, h, off):
        return buf.at[h, pl.ds(SLOT[off] * ROWS, ROWS), :]

    bufs = {"q": (q_all, Q_ROUTE), "d": (do_all, D_ROUTE)}

    def gather(tag, h, n):
        buf, route = bufs[tag]
        for o in layer(route, n):
            if not feeders(route, o):
                continue
            if o:
                recv(z_slot(buf, h, o), tag, (tag, h, o))
            for off in feeders(route, o):
                key = (tag, h, off if feeders(route, off) else "rest")
                dst = z_slot(buf, h, off)
                send(z_slot(buf, h, o), dst, tag, key, to_ctx=at_z(-route[off]))

    def gather_rest(tag, h):
        buf, route = bufs[tag]
        ends = [o for o in OFFS[1:] if not feeders(route, o)]
        recv(buf.at[h, pl.ds(0, len(ends) * ROWS), :], tag, (tag, h, "rest"))

    pieces = ((0, ROWS), (SECT, HCAP))

    def kv_first(h):
        for dy in (2, 1, 3):
            there = (NY - dy) % NY
            for start, size in pieces:
                src = kv_all.at[h, :, pl.ds(start, size), :]
                dst = kv_all.at[h, :, pl.ds(start + there * size, size), :]
                send(src, dst, "kv", ("kv", h), to_ctx=at_y(dy))

    def kv_second(h):
        recv(kv_all.at[h, :, pl.ds(0, (NY - 1) * (ROWS + HCAP)), :], "kv", ("kv", h))
        for start, size in pieces:
            src = kv_all.at[h, :, pl.ds(start, NY * size), :]
            dst = kv_all.at[h, :, pl.ds(start + NY * size, NY * size), :]
            send(src, dst, "kvs", ("kvs", h), to_ctx=sibling)

    def kv_rest(h):
        recv(kv_all.at[h, :, pl.ds(0, NY * (ROWS + HCAP)), :], "kvs", ("kvs", h))
        for i in range(KT // HDIM):
            rows = slice(i * HDIM, (i + 1) * HDIM)
            kt[h, :, rows] = kv_all[h, 0, rows, :].T
            vt[h, :, rows] = kv_all[h, 1, rows, :].T

    for dx in (2, 1, 3):
        there = (NX - dx) % NX
        send(g_ref, g_all.at[there], "g", ("g", there), to_head=at_x(dx))
    for h in range(HEADS):
        kv_first(h)
        gather("q", h, 0)

    row = lax.broadcasted_iota(jnp.int32, (HIST, CHUNK), 0)
    limit = jnp.zeros((HIST, CHUNK), jnp.int32)
    for dc in range(NC):
        for dy in range(NY):
            owner = (z * NY + lax.rem(y + dy, NY)) * NC + (core if dc == 0 else 1 - core)
            tokens = jnp.int32(0)
            for f in range(FMAX):
                level = lev_ref[f, owner]
                size = lax.shift_right_logical(jnp.int32(FTOK), 2 * level)
                tokens = tokens + jnp.where(f < cnt_ref[owner], size, 0)
            j = dc * NY + dy
            mine = (row >= j * HCAP) & (row < (j + 1) * HCAP)
            limit = jnp.where(mine, tokens + j * HCAP, limit)
    bias[...] = jnp.where(row < limit, 0.0, NEG_FILL)

    def w_cols(dx):
        return w_all[:, pl.ds(pl.multiple_of(at_x(dx) * OCOLS, OCOLS), OCOLS)]

    def cotangent():
        w_copy.wait()
        d_attn = dot_nt(g_ref[...], w_cols(0))
        for dx in (1, 3, 2):
            recv(g_all.at[dx], "g", ("g", dx))
            d_attn += dot_nt(g_all[dx], w_cols(dx))
        for h in range(HEADS):
            do_all[h, 0:ROWS, :] = d_attn[:, h * HDIM : (h + 1) * HDIM].astype(BF)

    def forward(h, pair):
        cols = slice(pair * CHUNK, (pair + 1) * CHUNK)
        query = q_all[h, cols, :]
        top = None
        for c in range(NCHUNK):
            rows = slice(c * CHUNK, (c + 1) * CHUNK)
            s = dot_nt(kv_all[h, 0, rows, :], query)
            if c == NCHUNK - 1:
                s = s + bias[...]
            s_scr[rows, :] = s
            part = jnp.max(s.reshape(CHUNK // 8, 8, CHUNK), axis=0)
            top = part if top is None else jnp.maximum(top, part)
        top = jnp.max(top, axis=0, keepdims=True) * SCALE2
        total = jnp.zeros((8, CHUNK), F32)
        for c in range(NCHUNK):
            rows = slice(c * CHUNK, (c + 1) * CHUNK)
            p = jnp.exp2(s_scr[rows, :] * SCALE2 - top)
            total += jnp.sum(p.reshape(CHUNK // 8, 8, CHUNK), axis=0)
            p_scr[h, rows, cols] = p.astype(BF)
        total = jnp.sum(total, axis=0, keepdims=True)
        o = dot_nn(vt[h], p_scr[h, :, cols])
        for i in range(2):
            half = slice(i * ROWS, (i + 1) * ROWS)
            slot = 2 * pair + i
            o_part[h, slot] = o[:, half].astype(BF)
            st[h, slot, 0:1, :] = top[:, half]
            st[h, slot, 1:2, :] = total[:, half]

    def s_send(tag, h, off, srcs, boxes, route):
        i = SLOT[off] - 1
        key = (tag, h, off - route[off])
        for n, (src, box) in enumerate(zip(srcs, boxes)):
            send(src, box.at[h, i], (tag, n), key + (n,), to_ctx=at_z(route[off]))

    def s_recv(tag, h, off, boxes, route):
        before = feeders(route, off)
        for n, box in enumerate(boxes):
            recv(box.at[h, pl.ds(0, len(before))], (tag, n), (tag, h, off, n))
        return [SLOT[o] - 1 for o in before]

    def stage(route, n):
        return layer(route, max(depth(route, o) for o in OFFS) + 1 - n)

    def merge(terms):
        peak = functools.reduce(jnp.maximum, [t[0] for t in terms])
        scales = [jnp.exp2(t[0] - peak) for t in terms]
        whole = sum(w * t[1] for w, t in zip(scales, terms))
        product = sum(w * t[2] for w, t in zip(scales, terms))
        return peak, whole, product

    def o_triple(h, slot):
        return st[h, slot, 0:1, :], st[h, slot, 1:2, :], o_part[h, slot].astype(F32)

    def o_arrived(h, off):
        boxes = s_recv("o", h, off, (o_in, st_in), O_ROUTE[h])
        return [(st_in[h, i, 0:1, :], st_in[h, i, 1:2, :], o_in[h, i].astype(F32)) for i in boxes]

    def o_stage(h, n):
        route = O_ROUTE[h]
        for off in stage(route, n):
            slot = SLOT[off]
            srcs = (o_part.at[h, slot], st.at[h, slot])
            if feeders(route, off):
                peak, whole, product = merge([o_triple(h, slot)] + o_arrived(h, off))
                st_mid[h, slot, 0:1, :] = peak
                st_mid[h, slot, 1:2, :] = whole
                o_mid[h, slot] = product.astype(BF)
                srcs = (o_mid.at[h, slot], st_mid.at[h, slot])
            s_send("o", h, off, srcs, (o_in, st_in), route)

    def o_finish(h):
        peak, whole, product = merge([o_triple(h, 0)] + o_arrived(h, 0))
        mine = (product / whole).T.astype(BF)
        at_all[h, 0] = mine
        for dx in (2, 1, 3):
            there = (NX - dx) % NX
            send(at_all.at[h, 0], at_all.at[h, there], "at", ("at", h), to_head=at_x(dx))
        both = mine.astype(F32) * do_all[h, 0:ROWS, :].astype(F32)
        delta = jnp.sum(both.T, axis=0, keepdims=True)
        ret[h, 0:1, :] = peak + jnp.log2(whole)
        ret[h, 1:2, :] = delta
        for off in OFFS[1:]:
            there = SLOT[-off]
            send(ret.at[h], ret_recv.at[h, there], "ret", ("ret", h), to_ctx=at_z(off))

    def settle(h):
        recv(ret_recv.at[h, pl.ds(1, NZ - 1)], "ret", ("ret", h))
        for slot in range(NZ):
            back = ret[h] if slot == 0 else ret_recv[h, slot]
            factor = jnp.exp2(st[h, slot, 0:1, :] - back[0:1])
            cd[h, 0:1, slot * ROWS : (slot + 1) * ROWS] = factor * back[1:2]
            rows = slice(slot * ROWS, (slot + 1) * ROWS)
            column = jnp.broadcast_to(factor, (ROWS, ROWS)).T
            dop[h, rows, :] = (do_all[h, rows, :].astype(F32) * column).astype(BF)

    def scores_back(h, chunks):
        for c in chunks:
            rows = slice(c * CHUNK, (c + 1) * CHUNK)
            value = kv_all[h, 1, rows, :]
            for pair in range(4):
                cols = slice(pair * CHUNK, (pair + 1) * CHUNK)
                dp = dot_nt(value, dop[h, cols, :])
                ds = p_scr[h, rows, cols].astype(F32) * (dp - cd[h, 0:1, cols])
                ds_scr[rows, cols] = ds.astype(BF)

    def keys_back(h, chunks):
        for c in chunks:
            rows = slice(c * CHUNK, (c + 1) * CHUNK)
            dkv_scr[h, rows, 0:HDIM] = dot_nn(ds_scr[rows, :], q_all[h]).astype(BF)
            dkv_scr[h, rows, HDIM : 2 * HDIM] = dot_nn(p_scr[h, rows, :], dop[h]).astype(BF)

    def queries_back(h):
        for pair in (3, 2, 1, 0):
            cols = slice(pair * CHUNK, (pair + 1) * CHUNK)
            dq = dot_nn(kt[h], ds_scr[:, cols])
            for i in range(2):
                dq_part[h, 2 * pair + i] = dq[:, i * ROWS : (i + 1) * ROWS].astype(BF)

    def dq_stage(h, n):
        route = DQ_ROUTE[h]
        for off in stage(route, n):
            slot = SLOT[off]
            src = dq_part.at[h, slot]
            if feeders(route, off):
                total = dq_part[h, slot].astype(F32)
                for i in s_recv("dq", h, off, (dq_in,), route):
                    total += dq_in[h, i].astype(F32)
                dq_mid[h, slot] = total.astype(BF)
                src = dq_mid.at[h, slot]
            s_send("dq", h, off, (src,), (dq_in,), route)

    def dq_finish(h):
        total = dq_part[h, 0].astype(F32)
        for i in s_recv("dq", h, 0, (dq_in,), DQ_ROUTE[h]):
            total += dq_in[h, i].astype(F32)
        gq_ref[:, h * HDIM : (h + 1) * HDIM] = (total * SCALE).T.astype(BF)

    def keys_to_sibling(h):
        src = dkv_scr.at[h, pl.ds(SECT // 2, SECT // 2)]
        send(src, r1_sec.at[h], "r1s", ("r1s", h), to_ctx=sibling)
        src = dkv_scr.at[h, pl.ds(SECT + HIST // 2, HIST // 2)]
        send(src, r1_hist.at[h], "r1h", ("r1h", h), to_ctx=sibling)

    def keys_along_y(h):
        recv(r1_sec.at[h], "r1s", ("r1s", h))
        recv(r1_hist.at[h], "r1h", ("r1h", h))
        for dy in (2, 1, 3, 0):
            there = (NY - dy) % NY
            for name, got, total, into, start, size in (
                ("r2s", r1_sec, t_sec, r2_sec, 0, ROWS),
                ("r2h", r1_hist, t_hist, r2_hist, SECT, HCAP),
            ):
                rows = slice(dy * size, (dy + 1) * size)
                own = dkv_scr[h, start + dy * size : start + (dy + 1) * size, :].astype(F32)
                total[h, rows, :] = (own + got[h, rows, :].astype(F32)).astype(BF)
                if dy:
                    src = total.at[h, pl.ds(dy * size, size)]
                    send(src, into.at[h, there], name, (name, h), to_ctx=at_y(dy))

    def keys_finish(h):
        cols = slice(h * HDIM, (h + 1) * HDIM)
        for name, total, into, size, k_out, v_out in (
            ("r2s", t_sec, r2_sec, ROWS, gk_ref, gv_ref),
            ("r2h", t_hist, r2_hist, HCAP, ghk_ref, ghv_ref),
        ):
            value = total[h, 0:size, :].astype(F32)
            recv(into.at[h, pl.ds(1, NY - 1)], name, (name, h))
            for dy in range(1, NY):
                value = value + into[h, dy].astype(F32)
            k_out[:, cols] = (value[:, 0:HDIM] * SCALE).astype(BF)
            v_out[:, cols] = value[:, HDIM : 2 * HDIM].astype(BF)

    def half(base):
        return pl.ds(pl.multiple_of(base + core * (OCOLS // 2), OCOLS // 2), OCOLS // 2)

    def w_first():
        for dx in (2, 1, 3):
            there = (NX - dx) % NX
            src = w_all.at[:, half(at_x(dx) * OCOLS)]
            send(src, w_far.at[there, :, half(0)], "w", ("w",), to_head=at_x(dx))

    def w_second():
        recv(w_far.at[pl.ds(1, NX - 1), :, half(0)], "w", ("w",))
        part = w_far.at[pl.ds(1, NX - 1), :, half(0)]
        send(part, part, "ws", ("ws",), to_ctx=sibling)

    def w_rest():
        recv(w_far.at[pl.ds(1, NX - 1), :, half(0)], "ws", ("ws",))

    def project(heads, first, last):
        rows = slice(heads[0] * HDIM, (heads[-1] + 1) * HDIM)
        total = None if first else acc[...]
        for h in heads:
            recv(at_all.at[h, pl.ds(1, NX - 1)], "at", ("at", h))
        for dx in (0, 1, 3, 2):
            left = jnp.concatenate([at_all[h, dx] for h in heads], axis=1)
            part = dot_nn(left, w_far[dx, rows, :] if dx else w_cols(0)[rows, :])
            total = part if total is None else total + part
        if last:
            out_ref[...] = total.astype(BF)
        else:
            acc[...] = total

    gather("q", 0, 1)
    kv_second(0)
    gather("q", 1, 1)
    gather("q", 2, 1)
    kv_rest(0)
    kv_second(1)
    gather_rest("q", 0)
    forward(0, 2)
    cotangent()
    gather("d", 0, 0)
    gather("d", 1, 0)
    forward(0, 3)
    kv_second(2)
    kv_rest(1)
    o_stage(0, 1)
    gather_rest("q", 1)
    forward(1, 2)
    gather("d", 2, 0)
    forward(1, 3)
    gather_rest("q", 2)
    kv_rest(2)
    gather("d", 0, 1)
    o_stage(1, 1)
    w_first()
    forward(0, 1)
    forward(0, 0)
    o_stage(0, 2)
    gather("d", 1, 1)
    forward(1, 1)
    forward(2, 3)
    gather("d", 2, 1)
    forward(2, 2)
    gather("d", 0, 2)
    o_stage(2, 1)
    forward(2, 0)
    forward(2, 1)
    forward(1, 0)
    o_finish(0)
    o_stage(1, 2)
    o_stage(2, 2)
    gather("d", 1, 2)
    gather_rest("d", 0)
    settle(0)
    scores_back(0, (0, 1))
    o_finish(1)
    gather("d", 2, 2)
    scores_back(0, (2, 3, 4))
    keys_back(0, (2, 3, 4))
    keys_to_sibling(0)
    o_finish(2)
    queries_back(0)
    dq_stage(0, 1)
    w_second()
    keys_back(0, (0, 1))
    gather_rest("d", 1)
    keys_along_y(0)
    settle(1)
    scores_back(1, (0, 1))
    keys_back(1, (0, 1))
    scores_back(1, (2, 3, 4))
    keys_back(1, (2, 3, 4))
    gather_rest("d", 2)
    queries_back(1)
    keys_to_sibling(1)
    dq_stage(1, 1)
    settle(2)
    scores_back(2, (0, 1))
    scores_back(2, (2, 3, 4))
    keys_along_y(1)
    queries_back(2)
    dq_stage(2, 1)
    keys_back(2, (2, 3, 4))
    keys_to_sibling(2)
    keys_back(2, (0, 1))
    dq_stage(1, 2)
    keys_along_y(2)
    dq_stage(2, 2)
    w_rest()
    dq_finish(0)
    keys_finish(1)
    project((0, 1), True, False)
    keys_finish(0)
    project((2,), False, True)
    dq_finish(1)
    keys_finish(2)
    dq_finish(2)

    seven = pl.ds(0, NZ - 1)
    for group, same_size in {
        "q": q_all.at[:, pl.ds(0, (NZ - 1) * ROWS), :],
        "d": do_all.at[:, pl.ds(0, (NZ - 1) * ROWS), :],
        "kv": kv_all.at[:, :, pl.ds(0, (NY - 1) * (ROWS + HCAP)), :],
        "kvs": kv_all.at[:, :, pl.ds(0, NY * (ROWS + HCAP)), :],
        "g": g_all.at[pl.ds(0, NX - 1)],
        "w": w_far.at[pl.ds(0, NX - 1), :, half(0)],
        "ws": w_far.at[pl.ds(0, NX - 1), :, half(0)],
        ("o", 0): o_in.at[:, seven],
        ("o", 1): st_in.at[:, seven],
        "ret": ret_recv.at[:, seven],
        "at": at_all.at[:, pl.ds(0, NX - 1)],
        ("dq", 0): dq_in.at[:, seven],
        "r1s": r1_sec,
        "r1h": r1_hist,
        "r2s": r2_sec.at[:, pl.ds(0, NY - 1)],
        "r2h": r2_hist.at[:, pl.ds(0, NY - 1)],
    }.items():
        remote(same_size, same_size, group, ("w",), sibling, None).wait_send()
    assert len(groups.names) <= N_SEND, len(groups.names)
    assert len(arrivals.names) <= N_RECV, len(arrivals.names)


def write_kernel(*refs):
    n = (len(refs) - 1) // 2
    sems = refs[-1]
    copies = [pltpu.make_async_copy(refs[i], refs[n + i], sems.at[i]) for i in range(n)]
    for copy in copies:
        copy.start()
    for copy in copies:
        copy.wait()


def write(arrays):
    n = len(arrays)
    return pl.pallas_call(
        write_kernel,
        out_shape=[jax.ShapeDtypeStruct(a.shape, a.dtype) for a in arrays],
        in_specs=[pl.BlockSpec(memory_space=pltpu.VMEM)] * n,
        out_specs=[pl.BlockSpec(memory_space=pl.ANY)] * n,
        scratch_shapes=[pltpu.SemaphoreType.DMA((n,))],
    )(*arrays)


def shards(sec_q, sec_k, sec_v, hist_k, hist_v, frame_levels, frame_counts, w_out, grad_out):
    vmem = pl.BlockSpec(memory_space=pltpu.VMEM)
    smem = pl.BlockSpec(memory_space=pltpu.SMEM)
    anywhere = pl.BlockSpec(memory_space=pl.ANY)
    box = (HEADS, NZ, HDIM, ROWS)
    scratch = [
        pltpu.VMEM((HEADS, QT, HDIM), BF),
        pltpu.VMEM((HEADS, 2, KT, HDIM), BF),
        pltpu.VMEM((HEADS, HDIM, KT), BF),
        pltpu.VMEM((HEADS, HDIM, KT), BF),
        pltpu.VMEM((WIDTH, NX * OCOLS), BF),
        pltpu.VMEM((NX, ROWS, OCOLS), BF),
        pltpu.VMEM((HEADS, QT, HDIM), BF),
        pltpu.VMEM((HEADS, QT, HDIM), BF),
        pltpu.VMEM((HIST, CHUNK), F32),
        pltpu.VMEM((KT, CHUNK), F32),
        pltpu.VMEM((HEADS, KT, QT), BF),
        pltpu.VMEM(box, BF),
        pltpu.VMEM((KT, QT), BF),
        pltpu.VMEM(box, BF),
        pltpu.VMEM((HEADS, KT, 2 * HDIM), BF),
        pltpu.VMEM((HEADS, NZ, 2, ROWS), F32),
        pltpu.VMEM((HEADS, 2, ROWS), F32),
        pltpu.VMEM((HEADS, NZ, 2, ROWS), F32),
        pltpu.VMEM((HEADS, 8, QT), F32),
        pltpu.VMEM(box, BF),
        pltpu.VMEM(box, BF),
        pltpu.VMEM((HEADS, NZ, 2, ROWS), F32),
        pltpu.VMEM((HEADS, NZ, 2, ROWS), F32),
        pltpu.VMEM(box, BF),
        pltpu.VMEM(box, BF),
        pltpu.VMEM((HEADS, SECT // 2, 2 * HDIM), BF),
        pltpu.VMEM((HEADS, HIST // 2, 2 * HDIM), BF),
        pltpu.VMEM((HEADS, SECT // 2, 2 * HDIM), BF),
        pltpu.VMEM((HEADS, HIST // 2, 2 * HDIM), BF),
        pltpu.VMEM((HEADS, NY, ROWS, 2 * HDIM), BF),
        pltpu.VMEM((HEADS, NY, HCAP, 2 * HDIM), BF),
        pltpu.VMEM((HEADS, NX, ROWS, HDIM), BF),
        pltpu.VMEM((NX, WIDTH, OCOLS), BF),
        pltpu.VMEM((ROWS, OCOLS), F32),
        pltpu.SemaphoreType.DMA((N_SEND,)),
        pltpu.SemaphoreType.DMA((N_RECV,)),
        pltpu.SemaphoreType.DMA(()),
    ]
    shapes = [
        jax.ShapeDtypeStruct((ROWS, OCOLS), BF),
        jax.ShapeDtypeStruct((ROWS, WIDTH), BF),
        jax.ShapeDtypeStruct((ROWS, WIDTH), BF),
        jax.ShapeDtypeStruct((ROWS, WIDTH), BF),
        jax.ShapeDtypeStruct((HCAP, WIDTH), BF),
        jax.ShapeDtypeStruct((HCAP, WIDTH), BF),
    ]
    results = pl.pallas_call(
        kernel,
        out_shape=shapes,
        in_specs=[vmem] * 5 + [smem] * 2 + [anywhere, vmem],
        out_specs=[vmem] * 6,
        scratch_shapes=scratch,
        compiler_params=pltpu.CompilerParams(
            collective_id=0, has_side_effects=True, vmem_limit_bytes=60 * 1024 * 1024
        ),
    )(sec_q, sec_k, sec_v, hist_k, hist_v, frame_levels.T, frame_counts, w_out, grad_out)
    return write(results)


def solution(mesh):
    both = P("ctx", "head")
    placed = (both, both, both, both, both, P(), P(), P("head", None), both)
    return jax.shard_map(
        shards, mesh=mesh, in_specs=placed, out_specs=(both,) * 6, check_vma=False
    )
```

```python
import functools
import math

import jax
import jax.numpy as jnp
from jax import lax
from jax.experimental import pallas as pl
from jax.experimental.pallas import tpu as pltpu
from jax.sharding import PartitionSpec as P

HDIM = 128
FTOK = 16
FMAX = 2
NEG_FILL = -1e30
MESH = pl.DeviceIdType.MESH

NZ, NY, NC, NX = 8, 4, 2, 4
HEADS = 3
ROWS = 128
HCAP = 32
QT = NZ * ROWS
SECT = NY * NC * ROWS
HIST = NY * NC * HCAP
KT = SECT + HIST
CHUNK = 256
NCHUNK = KT // CHUNK
WIDTH = HEADS * HDIM
OCOLS = 768
BF = jnp.bfloat16
F32 = jnp.float32

OFFS = (0, 1, -1, 2, -2, 3, -3, 4)
SLOT = {off: i for i, off in enumerate(OFFS)}
SLOT[-4] = SLOT[4]

DIRECT = {o: o for o in OFFS[1:]}
TWO = {4: 2, 3: 1, -3: -1, 2: 2, -2: -2, 1: 1, -1: -1}
THREE = {4: 2, 3: 1, -3: -1, 2: 1, -2: -1, 1: 1, -1: -1}
RING = {4: 1, 3: 1, -3: -1, 2: 1, -2: -1, 1: 1, -1: -1}


def feeders(route, off):
    return [o for o in OFFS[1:] if o - route[o] == off]


def depth(route, off):
    return 0 if off == 0 else 1 + depth(route, off - route[off])


def layer(route, n):
    return [o for o in OFFS if depth(route, o) == n]


SCALE = 1.0 / math.sqrt(HDIM)
SCALE2 = SCALE * math.log2(math.e)


def dot_nn(a, b):
    return lax.dot_general(a, b, (((1,), (0,)), ((), ())), preferred_element_type=F32)


def dot_nt(a, b):
    return lax.dot_general(a, b, (((1,), (1,)), ((), ())), preferred_element_type=F32)


class Sems:
    def __init__(self):
        self.names = {}

    def __call__(self, *name):
        return self.names.setdefault(name, len(self.names))


N_SEND, N_RECV = 16, 78
Q_ROUTE, D_ROUTE = TWO, THREE
O_ROUTE = (TWO, TWO, TWO)
DQ_ROUTE = (DIRECT, TWO, TWO)


def kernel(
    q_ref, k_ref, v_ref, hk_ref, hv_ref, lev_ref, cnt_ref, w_hbm, g_ref,
    out_ref, gq_ref, gk_ref, gv_ref, ghk_ref, ghv_ref,
    q_all, kv_all, kt, vt, w_all, g_all, do_all, dop, bias,
    s_scr, p_scr, o_part, ds_scr, dq_part, dkv_scr,
    st, ret, ret_recv, cd,
    o_mid, o_in, st_mid, st_in, dq_mid, dq_in,
    r1_sec, r1_hist, t_sec, t_hist, r2_sec, r2_hist,
    at_all, w_far, acc,
    send_sem, recv_sem, w_sem,
):
    ctx = lax.axis_index("ctx")
    x = lax.axis_index("head")
    core = lax.rem(ctx, NC)
    y = lax.rem(ctx // NC, NY)
    z = ctx // (NC * NY)
    way = 1 - 2 * core

    def at_z(off):
        return (lax.rem(z + off * way + 2 * NZ, NZ) * NY + y) * NC + core

    def at_y(dy):
        return (z * NY + lax.rem(y + dy, NY)) * NC + core

    def at_x(dx):
        return lax.rem(x + dx, NX)

    sibling = (z * NY + y) * NC + (1 - core)

    groups, arrivals = Sems(), Sems()

    def remote(src, dst, group, key, to_ctx, to_head):
        return pltpu.make_async_remote_copy(
            src_ref=src, dst_ref=dst,
            send_sem=send_sem.at[groups(group)], recv_sem=recv_sem.at[arrivals(*key)],
            device_id=(ctx if to_ctx is None else to_ctx, x if to_head is None else to_head),
            device_id_type=MESH,
        )

    def send(src, dst, group, key, to_ctx=None, to_head=None):
        remote(src, dst, group, key, to_ctx, to_head).start()

    def recv(same_size, group, key):
        remote(same_size, same_size, group, key, sibling, None).wait_recv()

    barrier = pltpu.get_barrier_semaphore()
    peers = [(at_z(o), x) for o in OFFS[1:]]
    peers += [(at_y(d), x) for d in range(1, NY)]
    peers += [(sibling, x)]
    peers += [(ctx, at_x(d)) for d in range(1, NX)]
    for peer in peers:
        pl.semaphore_signal(barrier, inc=1, device_id=peer, device_id_type=MESH)

    w_copy = pltpu.make_async_copy(w_hbm, w_all, w_sem)
    w_copy.start()
    for h in range(HEADS):
        cols = slice(h * HDIM, (h + 1) * HDIM)
        q_all[h, 0:ROWS, :] = q_ref[:, cols]
        kv_all[h, 0, 0:ROWS, :] = k_ref[:, cols]
        kv_all[h, 0, SECT : SECT + HCAP, :] = hk_ref[:, cols]
        kv_all[h, 1, 0:ROWS, :] = v_ref[:, cols]
        kv_all[h, 1, SECT : SECT + HCAP, :] = hv_ref[:, cols]

    pl.semaphore_wait(barrier, len(peers))

    def z_slot(buf, h, off):
        return buf.at[h, pl.ds(SLOT[off] * ROWS, ROWS), :]

    bufs = {"q": (q_all, Q_ROUTE), "d": (do_all, D_ROUTE)}

    def gather(tag, h, n):
        buf, route = bufs[tag]
        for o in layer(route, n):
            if not feeders(route, o):
                continue
            if o:
                recv(z_slot(buf, h, o), tag, (tag, h, o))
            for off in feeders(route, o):
                key = (tag, h, off if feeders(route, off) else "rest")
                dst = z_slot(buf, h, off)
                send(z_slot(buf, h, o), dst, tag, key, to_ctx=at_z(-route[off]))

    def gather_rest(tag, h):
        buf, route = bufs[tag]
        ends = [o for o in OFFS[1:] if not feeders(route, o)]
        recv(buf.at[h, pl.ds(0, len(ends) * ROWS), :], tag, (tag, h, "rest"))

    pieces = ((0, ROWS), (SECT, HCAP))

    def kv_first(h):
        for dy in (2, 1, 3):
            there = (NY - dy) % NY
            for start, size in pieces:
                src = kv_all.at[h, :, pl.ds(start, size), :]
                dst = kv_all.at[h, :, pl.ds(start + there * size, size), :]
                send(src, dst, "kv", ("kv", h), to_ctx=at_y(dy))

    def kv_second(h):
        recv(kv_all.at[h, :, pl.ds(0, (NY - 1) * (ROWS + HCAP)), :], "kv", ("kv", h))
        for start, size in pieces:
            src = kv_all.at[h, :, pl.ds(start, NY * size), :]
            dst = kv_all.at[h, :, pl.ds(start + NY * size, NY * size), :]
            send(src, dst, "kvs", ("kvs", h), to_ctx=sibling)

    def kv_rest(h):
        recv(kv_all.at[h, :, pl.ds(0, NY * (ROWS + HCAP)), :], "kvs", ("kvs", h))
        for i in range(KT // HDIM):
            rows = slice(i * HDIM, (i + 1) * HDIM)
            kt[h, :, rows] = kv_all[h, 0, rows, :].T
            vt[h, :, rows] = kv_all[h, 1, rows, :].T

    for dx in (2, 1, 3):
        there = (NX - dx) % NX
        send(g_ref, g_all.at[there], "g", ("g", there), to_head=at_x(dx))
    for h in range(HEADS):
        kv_first(h)
        gather("q", h, 0)

    row = lax.broadcasted_iota(jnp.int32, (HIST, CHUNK), 0)
    limit = jnp.zeros((HIST, CHUNK), jnp.int32)
    for dc in range(NC):
        for dy in range(NY):
            owner = (z * NY + lax.rem(y + dy, NY)) * NC + (core if dc == 0 else 1 - core)
            tokens = jnp.int32(0)
            for f in range(FMAX):
                level = lev_ref[f, owner]
                size = lax.shift_right_logical(jnp.int32(FTOK), 2 * level)
                tokens = tokens + jnp.where(f < cnt_ref[owner], size, 0)
            j = dc * NY + dy
            mine = (row >= j * HCAP) & (row < (j + 1) * HCAP)
            limit = jnp.where(mine, tokens + j * HCAP, limit)
    bias[...] = jnp.where(row < limit, 0.0, NEG_FILL)

    def w_cols(dx):
        return w_all[:, pl.ds(pl.multiple_of(at_x(dx) * OCOLS, OCOLS), OCOLS)]

    def cotangent():
        w_copy.wait()
        d_attn = dot_nt(g_ref[...], w_cols(0))
        for dx in (1, 3, 2):
            recv(g_all.at[dx], "g", ("g", dx))
            d_attn += dot_nt(g_all[dx], w_cols(dx))
        for h in range(HEADS):
            do_all[h, 0:ROWS, :] = d_attn[:, h * HDIM : (h + 1) * HDIM].astype(BF)

    def forward(h, pair):
        cols = slice(pair * CHUNK, (pair + 1) * CHUNK)
        query = q_all[h, cols, :]
        top = None
        for c in range(NCHUNK):
            rows = slice(c * CHUNK, (c + 1) * CHUNK)
            s = dot_nt(kv_all[h, 0, rows, :], query)
            if c == NCHUNK - 1:
                s = s + bias[...]
            s_scr[rows, :] = s
            part = jnp.max(s.reshape(CHUNK // 8, 8, CHUNK), axis=0)
            top = part if top is None else jnp.maximum(top, part)
        top = jnp.max(top, axis=0, keepdims=True) * SCALE2
        total = jnp.zeros((8, CHUNK), F32)
        for c in range(NCHUNK):
            rows = slice(c * CHUNK, (c + 1) * CHUNK)
            p = jnp.exp2(s_scr[rows, :] * SCALE2 - top)
            total += jnp.sum(p.reshape(CHUNK // 8, 8, CHUNK), axis=0)
            p_scr[h, rows, cols] = p.astype(BF)
        total = jnp.sum(total, axis=0, keepdims=True)
        o = dot_nn(vt[h], p_scr[h, :, cols])
        for i in range(2):
            half = slice(i * ROWS, (i + 1) * ROWS)
            slot = 2 * pair + i
            o_part[h, slot] = o[:, half].astype(BF)
            st[h, slot, 0:1, :] = top[:, half]
            st[h, slot, 1:2, :] = total[:, half]

    def s_send(tag, h, off, srcs, boxes, route):
        i = SLOT[off] - 1
        key = (tag, h, off - route[off])
        for n, (src, box) in enumerate(zip(srcs, boxes)):
            send(src, box.at[h, i], (tag, n), key + (n,), to_ctx=at_z(route[off]))

    def s_recv(tag, h, off, boxes, route):
        before = feeders(route, off)
        for n, box in enumerate(boxes):
            recv(box.at[h, pl.ds(0, len(before))], (tag, n), (tag, h, off, n))
        return [SLOT[o] - 1 for o in before]

    def stage(route, n):
        return layer(route, max(depth(route, o) for o in OFFS) + 1 - n)

    def merge(terms):
        peak = functools.reduce(jnp.maximum, [t[0] for t in terms])
        scales = [jnp.exp2(t[0] - peak) for t in terms]
        whole = sum(w * t[1] for w, t in zip(scales, terms))
        product = sum(w * t[2] for w, t in zip(scales, terms))
        return peak, whole, product

    def o_triple(h, slot):
        return st[h, slot, 0:1, :], st[h, slot, 1:2, :], o_part[h, slot].astype(F32)

    def o_arrived(h, off):
        boxes = s_recv("o", h, off, (o_in, st_in), O_ROUTE[h])
        return [(st_in[h, i, 0:1, :], st_in[h, i, 1:2, :], o_in[h, i].astype(F32)) for i in boxes]

    def o_stage(h, n):
        route = O_ROUTE[h]
        for off in stage(route, n):
            slot = SLOT[off]
            srcs = (o_part.at[h, slot], st.at[h, slot])
            if feeders(route, off):
                peak, whole, product = merge([o_triple(h, slot)] + o_arrived(h, off))
                st_mid[h, slot, 0:1, :] = peak
                st_mid[h, slot, 1:2, :] = whole
                o_mid[h, slot] = product.astype(BF)
                srcs = (o_mid.at[h, slot], st_mid.at[h, slot])
            s_send("o", h, off, srcs, (o_in, st_in), route)

    def o_finish(h):
        peak, whole, product = merge([o_triple(h, 0)] + o_arrived(h, 0))
        mine = (product / whole).T.astype(BF)
        at_all[h, 0] = mine
        for dx in (2, 1, 3):
            there = (NX - dx) % NX
            send(at_all.at[h, 0], at_all.at[h, there], "at", ("at", h), to_head=at_x(dx))
        both = mine.astype(F32) * do_all[h, 0:ROWS, :].astype(F32)
        delta = jnp.sum(both.T, axis=0, keepdims=True)
        ret[h, 0:1, :] = peak + jnp.log2(whole)
        ret[h, 1:2, :] = delta
        for off in OFFS[1:]:
            there = SLOT[-off]
            send(ret.at[h], ret_recv.at[h, there], "ret", ("ret", h), to_ctx=at_z(off))

    def settle(h):
        recv(ret_recv.at[h, pl.ds(1, NZ - 1)], "ret", ("ret", h))
        for slot in range(NZ):
            back = ret[h] if slot == 0 else ret_recv[h, slot]
            factor = jnp.exp2(st[h, slot, 0:1, :] - back[0:1])
            cd[h, 0:1, slot * ROWS : (slot + 1) * ROWS] = factor * back[1:2]
            rows = slice(slot * ROWS, (slot + 1) * ROWS)
            column = jnp.broadcast_to(factor, (ROWS, ROWS)).T
            dop[h, rows, :] = (do_all[h, rows, :].astype(F32) * column).astype(BF)

    def scores_back(h, chunks):
        for c in chunks:
            rows = slice(c * CHUNK, (c + 1) * CHUNK)
            value = kv_all[h, 1, rows, :]
            for pair in range(4):
                cols = slice(pair * CHUNK, (pair + 1) * CHUNK)
                dp = dot_nt(value, dop[h, cols, :])
                ds = p_scr[h, rows, cols].astype(F32) * (dp - cd[h, 0:1, cols])
                ds_scr[h % 2, rows, cols] = ds.astype(BF)

    def keys_back(h, chunks):
        for c in chunks:
            rows = slice(c * CHUNK, (c + 1) * CHUNK)
            dkv_scr[h, rows, 0:HDIM] = dot_nn(ds_scr[h % 2, rows, :], q_all[h]).astype(BF)
            dkv_scr[h, rows, HDIM : 2 * HDIM] = dot_nn(p_scr[h, rows, :], dop[h]).astype(BF)

    def queries_back(h):
        for pair in (3, 2, 1, 0):
            cols = slice(pair * CHUNK, (pair + 1) * CHUNK)
            dq = dot_nn(kt[h], ds_scr[h % 2, :, cols])
            for i in range(2):
                dq_part[h, 2 * pair + i] = dq[:, i * ROWS : (i + 1) * ROWS].astype(BF)

    def dq_stage(h, n):
        route = DQ_ROUTE[h]
        for off in stage(route, n):
            slot = SLOT[off]
            src = dq_part.at[h, slot]
            if feeders(route, off):
                total = dq_part[h, slot].astype(F32)
                for i in s_recv("dq", h, off, (dq_in,), route):
                    total += dq_in[h, i].astype(F32)
                dq_mid[h, slot] = total.astype(BF)
                src = dq_mid.at[h, slot]
            s_send("dq", h, off, (src,), (dq_in,), route)

    def dq_finish(h):
        total = dq_part[h, 0].astype(F32)
        for i in s_recv("dq", h, 0, (dq_in,), DQ_ROUTE[h]):
            total += dq_in[h, i].astype(F32)
        gq_ref[:, h * HDIM : (h + 1) * HDIM] = (total * SCALE).T.astype(BF)

    def keys_to_sibling(h):
        src = dkv_scr.at[h, pl.ds(SECT // 2, SECT // 2)]
        send(src, r1_sec.at[h], "r1s", ("r1s", h), to_ctx=sibling)
        src = dkv_scr.at[h, pl.ds(SECT + HIST // 2, HIST // 2)]
        send(src, r1_hist.at[h], "r1h", ("r1h", h), to_ctx=sibling)

    def keys_along_y(h):
        recv(r1_sec.at[h], "r1s", ("r1s", h))
        recv(r1_hist.at[h], "r1h", ("r1h", h))
        for dy in (2, 1, 3, 0):
            there = (NY - dy) % NY
            for name, got, total, into, start, size in (
                ("r2s", r1_sec, t_sec, r2_sec, 0, ROWS),
                ("r2h", r1_hist, t_hist, r2_hist, SECT, HCAP),
            ):
                rows = slice(dy * size, (dy + 1) * size)
                own = dkv_scr[h, start + dy * size : start + (dy + 1) * size, :].astype(F32)
                total[h, rows, :] = (own + got[h, rows, :].astype(F32)).astype(BF)
                if dy:
                    src = total.at[h, pl.ds(dy * size, size)]
                    send(src, into.at[h, there], name, (name, h), to_ctx=at_y(dy))

    def keys_finish(h):
        cols = slice(h * HDIM, (h + 1) * HDIM)
        for name, total, into, size, k_out, v_out in (
            ("r2s", t_sec, r2_sec, ROWS, gk_ref, gv_ref),
            ("r2h", t_hist, r2_hist, HCAP, ghk_ref, ghv_ref),
        ):
            value = total[h, 0:size, :].astype(F32)
            recv(into.at[h, pl.ds(1, NY - 1)], name, (name, h))
            for dy in range(1, NY):
                value = value + into[h, dy].astype(F32)
            k_out[:, cols] = (value[:, 0:HDIM] * SCALE).astype(BF)
            v_out[:, cols] = value[:, HDIM : 2 * HDIM].astype(BF)

    def half(base):
        return pl.ds(pl.multiple_of(base + core * (OCOLS // 2), OCOLS // 2), OCOLS // 2)

    def w_first():
        for dx in (2, 1, 3):
            there = (NX - dx) % NX
            src = w_all.at[:, half(at_x(dx) * OCOLS)]
            send(src, w_far.at[there, :, half(0)], "w", ("w",), to_head=at_x(dx))

    def w_second():
        recv(w_far.at[pl.ds(1, NX - 1), :, half(0)], "w", ("w",))
        part = w_far.at[pl.ds(1, NX - 1), :, half(0)]
        send(part, part, "ws", ("ws",), to_ctx=sibling)

    def w_rest():
        recv(w_far.at[pl.ds(1, NX - 1), :, half(0)], "ws", ("ws",))

    def project(heads, first, last):
        rows = slice(heads[0] * HDIM, (heads[-1] + 1) * HDIM)
        total = None if first else acc[...]
        for h in heads:
            recv(at_all.at[h, pl.ds(1, NX - 1)], "at", ("at", h))
        for dx in (0, 1, 3, 2):
            left = jnp.concatenate([at_all[h, dx] for h in heads], axis=1)
            part = dot_nn(left, w_far[dx, rows, :] if dx else w_cols(0)[rows, :])
            total = part if total is None else total + part
        if last:
            out_ref[...] = total.astype(BF)
        else:
            acc[...] = total

    gather("q", 0, 1)
    kv_second(0)
    gather("q", 1, 1)
    gather("q", 2, 1)
    kv_rest(0)
    kv_second(1)
    gather_rest("q", 0)
    forward(0, 2)
    cotangent()
    gather("d", 0, 0)
    gather("d", 1, 0)
    forward(0, 3)
    kv_second(2)
    kv_rest(1)
    o_stage(0, 1)
    gather_rest("q", 1)
    forward(1, 2)
    gather("d", 2, 0)
    forward(1, 3)
    gather_rest("q", 2)
    kv_rest(2)
    gather("d", 0, 1)
    o_stage(1, 1)
    w_first()
    forward(0, 1)
    forward(0, 0)
    o_stage(0, 2)
    gather("d", 1, 1)
    forward(1, 1)
    forward(2, 3)
    gather("d", 2, 1)
    forward(2, 2)
    gather("d", 0, 2)
    o_stage(2, 1)
    forward(2, 0)
    forward(2, 1)
    forward(1, 0)
    o_finish(0)
    o_stage(1, 2)
    o_stage(2, 2)
    gather("d", 1, 2)
    gather_rest("d", 0)
    settle(0)
    scores_back(0, (0, 1))
    o_finish(1)
    gather("d", 2, 2)
    scores_back(0, (2, 3, 4))
    keys_back(0, (2, 3, 4))
    keys_to_sibling(0)
    o_finish(2)
    queries_back(0)
    dq_stage(0, 1)
    w_second()
    keys_back(0, (0, 1))
    gather_rest("d", 1)
    keys_along_y(0)
    settle(1)
    scores_back(1, (0, 1))
    keys_back(1, (0, 1))
    scores_back(1, (2, 3, 4))
    keys_back(1, (2, 3, 4))
    gather_rest("d", 2)
    queries_back(1)
    keys_to_sibling(1)
    dq_stage(1, 1)
    settle(2)
    scores_back(2, (0, 1))
    scores_back(2, (2, 3, 4))
    keys_along_y(1)
    queries_back(2)
    dq_stage(2, 1)
    keys_back(2, (2, 3, 4))
    keys_to_sibling(2)
    keys_back(2, (0, 1))
    dq_stage(1, 2)
    keys_along_y(2)
    dq_stage(2, 2)
    w_rest()
    dq_finish(0)
    keys_finish(1)
    project((0, 1), True, False)
    keys_finish(0)
    project((2,), False, True)
    dq_finish(1)
    keys_finish(2)
    dq_finish(2)

    seven = pl.ds(0, NZ - 1)
    for group, same_size in {
        "q": q_all.at[:, pl.ds(0, (NZ - 1) * ROWS), :],
        "d": do_all.at[:, pl.ds(0, (NZ - 1) * ROWS), :],
        "kv": kv_all.at[:, :, pl.ds(0, (NY - 1) * (ROWS + HCAP)), :],
        "kvs": kv_all.at[:, :, pl.ds(0, NY * (ROWS + HCAP)), :],
        "g": g_all.at[pl.ds(0, NX - 1)],
        "w": w_far.at[pl.ds(0, NX - 1), :, half(0)],
        "ws": w_far.at[pl.ds(0, NX - 1), :, half(0)],
        ("o", 0): o_in.at[:, seven],
        ("o", 1): st_in.at[:, seven],
        "ret": ret_recv.at[:, seven],
        "at": at_all.at[:, pl.ds(0, NX - 1)],
        ("dq", 0): dq_in.at[:, seven],
        "r1s": r1_sec,
        "r1h": r1_hist,
        "r2s": r2_sec.at[:, pl.ds(0, NY - 1)],
        "r2h": r2_hist.at[:, pl.ds(0, NY - 1)],
    }.items():
        remote(same_size, same_size, group, ("w",), sibling, None).wait_send()
    assert len(groups.names) <= N_SEND, len(groups.names)
    assert len(arrivals.names) <= N_RECV, len(arrivals.names)


def write_kernel(*refs):
    n = (len(refs) - 1) // 2
    sems = refs[-1]
    copies = [pltpu.make_async_copy(refs[i], refs[n + i], sems.at[i]) for i in range(n)]
    for copy in copies:
        copy.start()
    for copy in copies:
        copy.wait()


def write(arrays):
    n = len(arrays)
    return pl.pallas_call(
        write_kernel,
        out_shape=[jax.ShapeDtypeStruct(a.shape, a.dtype) for a in arrays],
        in_specs=[pl.BlockSpec(memory_space=pltpu.VMEM)] * n,
        out_specs=[pl.BlockSpec(memory_space=pl.ANY)] * n,
        scratch_shapes=[pltpu.SemaphoreType.DMA((n,))],
    )(*arrays)


def shards(sec_q, sec_k, sec_v, hist_k, hist_v, frame_levels, frame_counts, w_out, grad_out):
    vmem = pl.BlockSpec(memory_space=pltpu.VMEM)
    smem = pl.BlockSpec(memory_space=pltpu.SMEM)
    anywhere = pl.BlockSpec(memory_space=pl.ANY)
    box = (HEADS, NZ, HDIM, ROWS)
    scratch = [
        pltpu.VMEM((HEADS, QT, HDIM), BF),
        pltpu.VMEM((HEADS, 2, KT, HDIM), BF),
        pltpu.VMEM((HEADS, HDIM, KT), BF),
        pltpu.VMEM((HEADS, HDIM, KT), BF),
        pltpu.VMEM((WIDTH, NX * OCOLS), BF),
        pltpu.VMEM((NX, ROWS, OCOLS), BF),
        pltpu.VMEM((HEADS, QT, HDIM), BF),
        pltpu.VMEM((HEADS, QT, HDIM), BF),
        pltpu.VMEM((HIST, CHUNK), F32),
        pltpu.VMEM((KT, CHUNK), F32),
        pltpu.VMEM((HEADS, KT, QT), BF),
        pltpu.VMEM(box, BF),
        pltpu.VMEM((2, KT, QT), BF),
        pltpu.VMEM(box, BF),
        pltpu.VMEM((HEADS, KT, 2 * HDIM), BF),
        pltpu.VMEM((HEADS, NZ, 2, ROWS), F32),
        pltpu.VMEM((HEADS, 2, ROWS), F32),
        pltpu.VMEM((HEADS, NZ, 2, ROWS), F32),
        pltpu.VMEM((HEADS, 8, QT), F32),
        pltpu.VMEM(box, BF),
        pltpu.VMEM(box, BF),
        pltpu.VMEM((HEADS, NZ, 2, ROWS), F32),
        pltpu.VMEM((HEADS, NZ, 2, ROWS), F32),
        pltpu.VMEM(box, BF),
        pltpu.VMEM(box, BF),
        pltpu.VMEM((HEADS, SECT // 2, 2 * HDIM), BF),
        pltpu.VMEM((HEADS, HIST // 2, 2 * HDIM), BF),
        pltpu.VMEM((HEADS, SECT // 2, 2 * HDIM), BF),
        pltpu.VMEM((HEADS, HIST // 2, 2 * HDIM), BF),
        pltpu.VMEM((HEADS, NY, ROWS, 2 * HDIM), BF),
        pltpu.VMEM((HEADS, NY, HCAP, 2 * HDIM), BF),
        pltpu.VMEM((HEADS, NX, ROWS, HDIM), BF),
        pltpu.VMEM((NX, WIDTH, OCOLS), BF),
        pltpu.VMEM((ROWS, OCOLS), F32),
        pltpu.SemaphoreType.DMA((N_SEND,)),
        pltpu.SemaphoreType.DMA((N_RECV,)),
        pltpu.SemaphoreType.DMA(()),
    ]
    shapes = [
        jax.ShapeDtypeStruct((ROWS, OCOLS), BF),
        jax.ShapeDtypeStruct((ROWS, WIDTH), BF),
        jax.ShapeDtypeStruct((ROWS, WIDTH), BF),
        jax.ShapeDtypeStruct((ROWS, WIDTH), BF),
        jax.ShapeDtypeStruct((HCAP, WIDTH), BF),
        jax.ShapeDtypeStruct((HCAP, WIDTH), BF),
    ]
    results = pl.pallas_call(
        kernel,
        out_shape=shapes,
        in_specs=[vmem] * 5 + [smem] * 2 + [anywhere, vmem],
        out_specs=[vmem] * 6,
        scratch_shapes=scratch,
        compiler_params=pltpu.CompilerParams(
            collective_id=0, has_side_effects=True, vmem_limit_bytes=60 * 1024 * 1024
        ),
    )(sec_q, sec_k, sec_v, hist_k, hist_v, frame_levels.T, frame_counts, w_out, grad_out)
    return write(results)


def solution(mesh):
    both = P("ctx", "head")
    placed = (both, both, both, both, both, P(), P(), P("head", None), both)
    return jax.shard_map(
        shards, mesh=mesh, in_specs=placed, out_specs=(both,) * 6, check_vma=False
    )
```
